256 devices in a mesh: seq: 64 (over y, z, core), head: 4 (over x).
Axes of the slice: x: 4, y: 4, z: 8, core: 2. Of those that a mesh axis runs over, the one named last changes fastest.
Arguments:
- queries: bfloat16 [49152, 4096], P(('seq', 'head')), may hold values from -4.6 to 4.6
- key_rows: bfloat16 [49152, 512], P(('seq', 'head')), may hold values from -4.6 to 4.6
- value_rows: bfloat16 [49152, 512], P(('seq', 'head')), may hold values from -6 to 6
- out_grad: bfloat16 [49152, 4096], P(('seq', 'head')), may hold values from -6 to 6
- mover_dest: int32 [3072], P('seq'), may hold values from 0 to 3071, as said below
- segment_ids: int32 [49152], P('seq'), may hold values from 0 to 6399, as said below
Outputs:
- attention_out: bfloat16 [49152, 4096], P('seq', 'head')
- query_grad: bfloat16 [49152, 4096], P('seq', 'head')
- key_grad: bfloat16 [49152, 512], P('seq', 'head')
- value_grad: bfloat16 [49152, 512], P('seq', 'head')
The draws below stay inside these ranges and needn't reach their ends.
Inputs may be any that keep to these rules, and one draw needn't show every extreme that they name: `mover_dest`: each value names the shard (value // 48) and the block slot (value % 48) that receive one of the last 48 blocks of 4 rows of an owner's 768 rows; every value occurs once. One owner sends at most 3 blocks to one shard, and exactly 3 to some shard. `segment_ids`: equal values mark one completion, a run of consecutive rows inside one shard of 768 rows; values never fall along the rows. From row 576 of each shard on, each block of 4 rows begins a new completion.
All inputs are finite; a program needn't handle non-finite values.
Results may differ from the reference program's by a relative error of at most 0.0052.
Values may be sent and summed in bfloat16 or wider, within the bound.
No kernel may reach another device: no remote copies, remote signals or barrier semaphores. Data moves between devices by JAX's collectives and lax.ppermute only.
A program may use at most 128 MiB of HBM per device.

```python
import math
import jax
import jax.numpy as jnp
from jax import lax

HQ = 32
HK = 4
DH = 128
BLK = 4
CAPB = 3
SHARD = 768
TOKENS = 49152
MOVERS = 48
N_HEAD = 4


def draw_key_rows(key, part):
    folded = jax.random.fold_in(key, 11)
    shape = (TOKENS, HK * DH)
    drawn = jnp.clip(jax.random.normal(folded, shape, jnp.float32), -4.6, 4.6)
    return drawn.astype(jnp.bfloat16)


def draw_queries(key, part):
    folded = jax.random.fold_in(key, 13)
    shape = (TOKENS, HQ * DH)
    drawn = jnp.clip(jax.random.normal(folded, shape, jnp.float32), -4.6, 4.6)
    return drawn.astype(jnp.bfloat16)


def draw_mover_dest(key, part):
    folded = jax.random.fold_in(key, 23)
    shard_count = TOKENS // SHARD
    group_count = shard_count // 2
    first_perm = jax.random.permutation(jax.random.fold_in(folded, 1), shard_count)
    second_perm = jax.random.permutation(jax.random.fold_in(folded, 2), shard_count)
    offsets = jnp.arange(group_count) + 1
    targets = first_perm[(second_perm[:, None] + offsets[None, :]) % shard_count]
    group_order = jax.random.permutation(jax.random.fold_in(folded, 3), group_count)
    multiple = jnp.where(group_order < group_count // 4, CAPB, 1)
    group_of_block = jnp.repeat(jnp.arange(group_count), multiple, total_repeat_length=MOVERS)

    def shuffle_blocks(subkey):
        return jax.random.permutation(subkey, MOVERS)
    shuffles = jax.vmap(shuffle_blocks)(jax.random.split(jax.random.fold_in(folded, 4), shard_count))
    block_group = group_of_block[shuffles]
    block_target = jnp.take_along_axis(targets, block_group, axis=1).reshape(-1)
    order = jnp.argsort(block_target, stable=True)
    positions = jnp.arange(shard_count * MOVERS)
    ranking = jnp.zeros_like(block_target).at[order].set(positions - block_target[order] * MOVERS)
    slot_perms = jax.vmap(shuffle_blocks)(jax.random.split(jax.random.fold_in(folded, 5), shard_count))
    slots = slot_perms[block_target, ranking]
    return (block_target * MOVERS + slots).astype(jnp.int32)


def draw_segment_ids(key, part):
    folded = jax.random.fold_in(key, 37)
    shard_count = TOKENS // SHARD
    stay_rows = SHARD - MOVERS * BLK
    places = jnp.arange(SHARD)

    def pick_cuts(subkey):
        return jax.random.permutation(subkey, stay_rows - 8)[:3] + 8
    cuts = jax.vmap(pick_cuts)(jax.random.split(folded, shard_count))
    starts = (places[None, :] == 0) | jnp.any(places[None, :, None] == cuts[:, None, :], axis=-1)
    tail_place = places - stay_rows
    block_start = (tail_place >= 0) & (tail_place % BLK == 0)
    inner = jax.random.randint(jax.random.fold_in(folded, 1), (shard_count, MOVERS), 1, max(BLK, 2))
    block_number = jnp.maximum(tail_place, 0) // BLK
    picked = inner[:, block_number]
    extra = (tail_place[None, :] >= 0) & (tail_place[None, :] % BLK == picked)
    starts = starts | block_start[None, :] | extra
    return (jnp.cumsum(starts.reshape(-1).astype(jnp.int32)) - 1).astype(jnp.int32)


def steps_of(rng, shape, shards, least, high):
    factor_of, own = 1.0, jax.random.fold_in(rng, 6)
    for dim, shards_of in shards:
        draws = jnp.exp(jax.random.uniform(jax.random.fold_in(own, dim), (shards_of,), jnp.float32, least / len(shards), high / len(shards)))
        factor_of = factor_of * jnp.repeat(draws, shape[dim] // shards_of).reshape([-1 if axis == dim else 1 for axis in range(len(shape))])
    return factor_of


def normal_values(stream_key, shape, deviation, most, cuts=(), kind=jnp.bfloat16):
    entries = deviation * jax.random.normal(stream_key, shape, jnp.float32)
    if cuts:
        entries = entries * steps_of(stream_key, shape, cuts, -0.22, 0.18)
    return jnp.clip(entries, -most, most).astype(kind)


def setup_inputs(seed: int = 0) -> dict:
    keys = jax.random.split(jax.random.key(seed), 7)
    queries = draw_queries(jax.random.fold_in(keys[6], 71), 0)
    key_rows = draw_key_rows(jax.random.fold_in(keys[6], 71), 0)
    value_rows = normal_values(keys[2], (TOKENS, HK * DH), 1.0, 6.0, ((0, 256),))
    out_grad = normal_values(keys[3], (TOKENS, HQ * DH), 1.0, 6.0, ((0, 256),))
    mover_dest = draw_mover_dest(jax.random.fold_in(keys[6], 71), 0)
    segment_ids = draw_segment_ids(jax.random.fold_in(keys[6], 71), 0)
    return dict(queries=queries, key_rows=key_rows, value_rows=value_rows, out_grad=out_grad, mover_dest=mover_dest, segment_ids=segment_ids)


neg_large = -1e+30

def attend_shard(query_part, key_part, value_part, grad_part, segments, head_dim):
    row_count = query_part.shape[0]
    shared_heads = key_part.shape[1] // head_dim
    group_size = query_part.shape[1] // head_dim // shared_heads
    query_heads = query_part.reshape(row_count, shared_heads, group_size, head_dim).astype(jnp.float32)
    key_heads = key_part.reshape(row_count, shared_heads, head_dim).astype(jnp.float32)
    value_heads = value_part.reshape(row_count, shared_heads, head_dim).astype(jnp.float32)
    grad_heads = grad_part.reshape(row_count, shared_heads, group_size, head_dim).astype(jnp.float32)
    inv_root = 1.0 / math.sqrt(head_dim)
    block_rows = min(768, row_count)
    places = jnp.arange(row_count, dtype=jnp.int32)
    key_total = jnp.zeros((row_count, shared_heads, head_dim), jnp.float32)
    value_total = jnp.zeros((row_count, shared_heads, head_dim), jnp.float32)
    outputs = []
    query_grads = []
    for first_row in range(0, row_count, block_rows):
        query_block = query_heads[first_row:first_row + block_rows]
        grad_block = grad_heads[first_row:first_row + block_rows]
        allowed = (segments[first_row:first_row + block_rows, None] == segments[None, :]) & (places[None, :] <= places[first_row:first_row + block_rows, None])
        scores = jnp.einsum('qkgd,pkd->kgqp', query_block, key_heads) * inv_root
        scores = jnp.where(allowed[None, None], scores, neg_large)
        highest = lax.optimization_barrier(jnp.max(scores, axis=-1, keepdims=True))
        weights = jnp.exp(scores - highest)
        softmaxed = weights / lax.optimization_barrier(jnp.sum(weights, axis=-1, keepdims=True))
        probs_low = softmaxed.astype(jnp.bfloat16).astype(jnp.float32)
        attended = jnp.einsum('kgqp,pkd->qkgd', probs_low, value_heads)
        outputs.append(attended.astype(jnp.bfloat16).reshape(block_rows, -1))
        grad_probs = jnp.einsum('qkgd,pkd->kgqp', grad_block, value_heads)
        centre = lax.optimization_barrier(jnp.sum(softmaxed * grad_probs, axis=-1, keepdims=True))
        grad_scores = (softmaxed * (grad_probs - centre) * inv_root).astype(jnp.bfloat16).astype(jnp.float32)
        query_grads.append(jnp.einsum('kgqp,pkd->qkgd', grad_scores, key_heads).astype(jnp.bfloat16).reshape(block_rows, -1))
        key_total = key_total + jnp.einsum('kgqp,qkgd->pkd', grad_scores, query_block)
        value_total = value_total + jnp.einsum('kgqp,qkgd->pkd', probs_low, grad_block)
    return (jnp.concatenate(outputs, axis=0), jnp.concatenate(query_grads, axis=0), key_total.astype(jnp.bfloat16).reshape(row_count, -1), value_total.astype(jnp.bfloat16).reshape(row_count, -1))

def reference(queries, key_rows, value_rows, out_grad, mover_dest, segment_ids):
    shard_count = TOKENS // SHARD
    tail_start = SHARD - MOVERS * BLK

    def pack_rows(member):
        column_count = member.shape[1]
        shard_grid = member.reshape(shard_count, SHARD, column_count)
        moving = shard_grid[:, tail_start:].reshape(shard_count * MOVERS, BLK, column_count)
        placed = jnp.zeros_like(moving).at[mover_dest].set(moving)
        return jnp.concatenate([shard_grid[:, :tail_start], placed.reshape(shard_count, MOVERS * BLK, column_count)], axis=1)
    packed = [pack_rows(member) for member in (queries, key_rows, value_rows, out_grad)]
    segment_grid = segment_ids.reshape(shard_count, SHARD)

    def one_item(item_index):
        shard_index = item_index // N_HEAD
        group_index = item_index % N_HEAD
        pieces = []
        for shard_grid in packed:
            column_count = shard_grid.shape[2] // N_HEAD
            shard_rows = lax.dynamic_index_in_dim(shard_grid, shard_index, 0, keepdims=False)
            pieces.append(lax.dynamic_slice_in_dim(shard_rows, (group_index * column_count).astype(jnp.int32), column_count, 1))
        segments = lax.dynamic_index_in_dim(segment_grid, shard_index, 0, keepdims=False)
        return attend_shard(pieces[0], pieces[1], pieces[2], pieces[3], segments, DH)
    results = lax.map(one_item, jnp.arange(shard_count * N_HEAD, dtype=jnp.int32))
    finished = []
    for stacked in results:
        column_count = stacked.shape[2]
        grouped = stacked.reshape(shard_count, N_HEAD, SHARD, column_count).transpose(0, 2, 1, 3)
        finished.append(grouped.reshape(TOKENS, N_HEAD * column_count))
    return (finished[0], finished[1], finished[2], finished[3])
```

```python
import functools
import math

import jax
import jax.numpy as jnp
from jax import lax
from jax.experimental import pallas as pl
from jax.experimental.pallas import tpu as pltpu
from jax.sharding import PartitionSpec as P

DH = 128
GROUP = 8
QW = GROUP * DH
ROWS = 768
QUART = 192
STAY = 576
BLK = 4
NBLK = 48
SEQ = 64
SLOT = 56
WIDE = 2 * QW + 2 * DH
INV = 1.0 / math.sqrt(DH)
NEG = -1e30
F32 = jnp.float32
BF16 = jnp.bfloat16
VMEM_LIMIT = 56 * 1024 * 1024


def params():
    return pltpu.CompilerParams(vmem_limit_bytes=VMEM_LIMIT)


def swap_groups(x):
    sub = lax.broadcasted_iota(jnp.int32, x.shape, 1)
    grp = lax.broadcasted_iota(jnp.int32, x.shape, 2) // 16
    for bit in (1, 2, 4):
        s_on = (sub & bit) != 0
        l_on = (grp & bit) != 0
        up = pltpu.roll(pltpu.roll(x, 8 - bit, 1), 16 * bit, 2)
        down = pltpu.roll(pltpu.roll(x, bit, 1), 128 - 16 * bit, 2)
        x = jnp.where(s_on == l_on, x, jnp.where(l_on, up, down))
    return x


def pack_kernel(q_ref, k_ref, v_ref, g_ref, plan_ref, lo_ref, hi_ref, qs, ks, small):
    half = SEQ // 2
    ks[0] = k_ref[...].astype(F32)
    ks[1] = v_ref[...].astype(F32)
    pieces = []
    for r in range(8):
        rows = ks[r // 4, pl.ds(r % 4, NBLK, stride=BLK), :]
        pieces.append(rows.reshape(6, 8, DH))
    mixed = swap_groups(jnp.concatenate(pieces, axis=0))
    small[...] = jnp.zeros_like(small)
    for r in range(8):
        for b in range(6):
            small[pl.ds(r * 8, 8), b, :] = mixed[r * 6 + b]
    plan = plan_ref[...]
    small[:, 6, :] = jnp.broadcast_to((plan // 64).astype(F32), (SEQ, DH))
    small[:, 7, :] = jnp.broadcast_to((plan % 64).astype(F32), (SEQ, DH))
    for src, dst, first in ((q_ref, lo_ref, 0), (g_ref, hi_ref, half)):
        for n in range(GROUP):
            qs[n] = src[:, n * DH : (n + 1) * DH].astype(F32)
            for t in range(BLK):
                rows = qs[n, pl.ds(t, NBLK, stride=BLK), :]
                dst[t * GROUP + n, 0:NBLK, :] = rows.astype(BF16)
        dst[:, NBLK:SLOT, :] = small[pl.ds(first, half)].astype(BF16)


def pack_tail(queries, key_rows, value_rows, out_grad, plan_row, group):
    half = jax.ShapeDtypeStruct((SEQ // 2, SLOT, DH), BF16)
    return pl.pallas_call(
        pack_kernel,
        grid=(1,),
        in_specs=[
            pl.BlockSpec((QUART, QW), lambda i: (0, group)),
            pl.BlockSpec((QUART, DH), lambda i: (0, group)),
            pl.BlockSpec((QUART, DH), lambda i: (0, group)),
            pl.BlockSpec((QUART, QW), lambda i: (0, group)),
            pl.BlockSpec((1, DH), lambda i: (0, 0)),
        ],
        out_specs=[pl.BlockSpec((SEQ // 2, SLOT, DH), lambda i: (0, 0, 0))] * 2,
        out_shape=[half, half],
        scratch_shapes=[
            pltpu.VMEM((GROUP, QUART, DH), F32),
            pltpu.VMEM((2, QUART, DH), F32),
            pltpu.VMEM((SEQ, 8, DH), F32),
        ],
        compiler_params=params(),
        cost_estimate=pl.CostEstimate(flops=0, bytes_accessed=2_000_000, transcendentals=0),
        name="pack_tail",
    )(queries, key_rows, value_rows, out_grad, plan_row)


def slice_kernel(me_ref, q_ref, k_ref, v_ref, g_ref, o_ref):
    o_ref[:, 0:QW] = q_ref[...]
    o_ref[:, QW : 2 * QW] = g_ref[...]
    o_ref[:, 2 * QW : 2 * QW + DH] = k_ref[...]
    o_ref[:, 2 * QW + DH : WIDE] = v_ref[...]


def slice_group(queries, key_rows, value_rows, out_grad, group):
    column = lambda i, g: (0, g[0])
    return pl.pallas_call(
        slice_kernel,
        grid_spec=pltpu.PrefetchScalarGridSpec(
            num_scalar_prefetch=1,
            grid=(1,),
            in_specs=[
                pl.BlockSpec((QUART, QW), column),
                pl.BlockSpec((QUART, DH), column),
                pl.BlockSpec((QUART, DH), column),
                pl.BlockSpec((QUART, QW), column),
            ],
            out_specs=pl.BlockSpec((QUART, WIDE), lambda i, g: (0, 0)),
        ),
        out_shape=jax.ShapeDtypeStruct((QUART, WIDE), BF16),
        compiler_params=params(),
        cost_estimate=pl.CostEstimate(flops=0, bytes_accessed=1_800_000, transcendentals=0),
        name="slice_group",
    )(group.reshape(1), queries, key_rows, value_rows, out_grad)


TILE = 384


def route_kernel(in_ref, out_ref, xs, low, line, sel):
    count = SEQ * NBLK
    col = lax.broadcasted_iota(jnp.int32, (1, count), 1).astype(F32)
    owner = jnp.floor((col + 0.5) * (1.0 / NBLK))
    place = col - owner * NBLK
    pick = (lax.broadcasted_iota(jnp.int32, (DH, count), 0).astype(F32) == place).astype(BF16)
    mine = lax.broadcasted_iota(jnp.int32, (SEQ, count), 0).astype(F32) == owner
    tail = in_ref[:, NBLK:SLOT, :].astype(F32)
    for which, row in ((0, 6), (1, 7)):
        spread = jnp.dot(tail[:, row, :].astype(BF16), pick, preferred_element_type=F32)
        line[which : which + 1, :] = jnp.sum(jnp.where(mine, spread, 0.0), axis=0, keepdims=True)
    low[...] = (
        lax.broadcasted_iota(jnp.int32, (64, count), 0).astype(F32) == line[1:2, :]
    ).astype(BF16)

    lane = lax.broadcasted_iota(jnp.int32, (NBLK, DH), 1) // 16
    sub = lax.broadcasted_iota(jnp.int32, (NBLK, DH), 0) % 8
    here = lane == sub
    fold = (
        lax.broadcasted_iota(jnp.int32, (DH, DH), 0) % 16
        == lax.broadcasted_iota(jnp.int32, (DH, DH), 1) % 16
    ).astype(BF16)
    for s in range(SEQ):
        xs[s * NBLK : (s + 1) * NBLK, 0:DH] = in_ref[s, 0:NBLK, :]
        rows = [jnp.broadcast_to(tail[s, b : b + 1, :], (8, DH)) for b in range(6)]
        wide = jnp.where(here, jnp.concatenate(rows, axis=0), 0.0).astype(BF16)
        xs[s * NBLK : (s + 1) * NBLK, DH : 2 * DH] = jnp.dot(
            wide, fold, preferred_element_type=F32
        ).astype(BF16)

    def step(i, carry):
        for k in range(TILE // 64):
            high = (i * (TILE // 64) + k).astype(F32)
            row = jnp.where(line[0:1, :] == high, 1.0, 0.0).astype(BF16)
            sel[k * 64 : (k + 1) * 64, :] = low[...] * row
        got = jnp.dot(sel[...], xs[...], preferred_element_type=F32)
        for d in range(TILE // NBLK):
            part = got[d * NBLK : (d + 1) * NBLK]
            shard = i * (TILE // NBLK) + d
            out_ref[shard, 0:NBLK, :] = part[:, 0:DH].astype(BF16)
            kept = jnp.where(here, part[:, DH : 2 * DH], 0.0)
            sums = [jnp.sum(kept[b * 8 : b * 8 + 8], axis=0, keepdims=True) for b in range(6)]
            sums.append(jnp.zeros((2, DH), F32))
            out_ref[shard, NBLK:SLOT, :] = jnp.concatenate(sums, axis=0).astype(BF16)
        return carry

    lax.fori_loop(0, count // TILE, step, 0)


def route(slots):
    count = SEQ * NBLK
    shape = (SEQ, SLOT, DH)
    return pl.pallas_call(
        route_kernel,
        in_specs=[pl.BlockSpec(memory_space=pltpu.VMEM)],
        out_specs=pl.BlockSpec(memory_space=pltpu.VMEM),
        out_shape=jax.ShapeDtypeStruct(shape, BF16),
        scratch_shapes=[
            pltpu.VMEM((count, 2 * DH), BF16),
            pltpu.VMEM((64, count), BF16),
            pltpu.VMEM((8, count), F32),
            pltpu.VMEM((TILE, count), BF16),
        ],
        compiler_params=params(),
        cost_estimate=pl.CostEstimate(
            flops=2 * count * count * 2 * DH, bytes_accessed=2_000_000, transcendentals=0
        ),
        name="route",
    )(slots)


def dot(a, b, dims):
    return lax.dot_general(a, b, (dims, ((), ())), preferred_element_type=F32)


NT = ((1,), (1,))
NN = ((1,), (0,))
TN = ((0,), (0,))


def attend(q, g, k, v, allowed):
    scores = jnp.where(allowed, dot(q, k, NT) * INV, NEG)
    weights = jnp.exp(scores - jnp.max(scores, axis=-1, keepdims=True))
    probs = weights * (1.0 / jnp.sum(weights, axis=-1, keepdims=True))
    probs_low = probs.astype(BF16)
    out = dot(probs_low, v, NN).astype(BF16)
    grad_probs = dot(g, v, NT)
    centre = jnp.sum(probs * grad_probs, axis=-1, keepdims=True)
    grad_scores = (probs * (grad_probs - centre) * INV).astype(BF16)
    dq = dot(grad_scores, k, NN).astype(BF16)
    return out, dq, dot(grad_scores, q, TN), dot(probs_low, g, TN)


def causal(seg_col, seg_row, first):
    rows, cols = seg_col.shape[0], seg_row.shape[1]
    i = lax.broadcasted_iota(jnp.int32, (rows, cols), 0) + first
    j = lax.broadcasted_iota(jnp.int32, (rows, cols), 1)
    return (seg_col == seg_row) & (j <= i)


def stay_kernel(
    me_ref, q_any, k_any, v_any, g_any, plus, minus, two, relay, col_ref, row_ref,
    out_ref, dq_ref, dk_ref, dv_ref, rows, dk, dv, sems,
):
    n = pl.program_id(0)
    me = me_ref[0]

    @pl.when(n == 0)
    def _():
        def fetch(src, part):
            pltpu.make_async_copy(src, rows.at[pl.ds(part * QUART, QUART), :], sems.at[part]).start()

        wide = pl.ds(pl.multiple_of(me * QW, QW), QW)
        thin = pl.ds(pl.multiple_of(me * DH, DH), DH)

        def own(part):
            there = pl.ds(part * QUART, QUART)
            pltpu.make_async_copy(q_any.at[:, wide], rows.at[there, 0:QW], sems.at[part]).start()
            pltpu.make_async_copy(g_any.at[:, wide], rows.at[there, QW : 2 * QW], sems.at[part]).start()
            pltpu.make_async_copy(k_any.at[:, thin], rows.at[there, 2 * QW : 2 * QW + DH], sems.at[part]).start()
            pltpu.make_async_copy(v_any.at[:, thin], rows.at[there, 2 * QW + DH : WIDE], sems.at[part]).start()

        @pl.when(me == 0)
        def _():
            own(0)
            fetch(minus, 1)
            fetch(two, 2)

        @pl.when(me == 1)
        def _():
            fetch(plus, 0)
            own(1)
            fetch(minus, 2)

        @pl.when(me == 2)
        def _():
            fetch(two, 0)
            fetch(plus, 1)
            own(2)

        @pl.when(me == 3)
        def _():
            fetch(minus, 0)
            fetch(relay, 1)
            fetch(plus, 2)

        for part in range(3):
            pltpu.make_async_copy(plus, rows.at[pl.ds(part * QUART, QUART), :], sems.at[part]).wait()
        dk[...] = jnp.zeros_like(dk)
        dv[...] = jnp.zeros_like(dv)

    q_at = pl.ds(pl.multiple_of(n * DH, DH), DH)
    g_at = pl.ds(pl.multiple_of(QW + n * DH, DH), DH)
    for part in range(3):
        there = pl.ds(part * QUART, QUART)
        width = (part + 1) * QUART
        k = rows[0:width, 2 * QW : 2 * QW + DH]
        v = rows[0:width, 2 * QW + DH : WIDE]
        allowed = causal(col_ref[there, :], row_ref[:, 0:width], part * QUART)
        out, dq, dk_part, dv_part = attend(rows[there, q_at], rows[there, g_at], k, v, allowed)
        out_ref[there, :] = out
        dq_ref[there, :] = dq
        dk[0:width, :] += dk_part
        dv[0:width, :] += dv_part

    @pl.when(n == GROUP - 1)
    def _():
        dk_ref[...] = dk[...].astype(BF16)
        dv_ref[...] = dv[...].astype(BF16)


OUT_SHAPES = [
    jax.ShapeDtypeStruct((ROWS, QW), BF16),
    jax.ShapeDtypeStruct((ROWS, QW), BF16),
    jax.ShapeDtypeStruct((ROWS, DH), BF16),
    jax.ShapeDtypeStruct((ROWS, DH), BF16),
]


def attend_stay(me, held, received, seg_col, seg_row):
    any_spec = pl.BlockSpec(memory_space=pl.ANY)
    return pl.pallas_call(
        stay_kernel,
        grid_spec=pltpu.PrefetchScalarGridSpec(
            num_scalar_prefetch=1,
            grid=(GROUP,),
            in_specs=[any_spec] * 8
            + [
                pl.BlockSpec((STAY, 1), lambda n, m: (0, 0)),
                pl.BlockSpec((1, ROWS), lambda n, m: (0, 0)),
            ],
            out_specs=[
                pl.BlockSpec((STAY, DH), lambda n, m: (0, n)),
                pl.BlockSpec((STAY, DH), lambda n, m: (0, n)),
                pl.BlockSpec((STAY, DH), lambda n, m: (0, 0)),
                pl.BlockSpec((STAY, DH), lambda n, m: (0, 0)),
            ],
            scratch_shapes=[
                pltpu.VMEM((STAY, WIDE), BF16),
                pltpu.VMEM((STAY, DH), F32),
                pltpu.VMEM((STAY, DH), F32),
                pltpu.SemaphoreType.DMA((3,)),
            ],
        ),
        out_shape=OUT_SHAPES,
        compiler_params=params(),
        cost_estimate=pl.CostEstimate(
            flops=6 * 2 * GROUP * STAY * STAY * DH,
            bytes_accessed=6_000_000,
            transcendentals=GROUP * STAY * STAY,
        ),
        name="attend_stay",
    )(me.reshape(1), *held, *received, seg_col, seg_row)


def tail_kernel(
    slots, col_ref, row_ref, a0, a1, a2, a3, out_ref, dq_ref, dk_ref, dv_ref, qs, gs, ks, small
):
    for t in range(BLK):
        for n in range(GROUP):
            there = pl.ds(t, NBLK, stride=BLK)
            qs[n, there, :] = slots[t * GROUP + n, 0:NBLK, :].astype(F32)
            gs[n, there, :] = slots[SEQ // 2 + t * GROUP + n, 0:NBLK, :].astype(F32)
    small[...] = slots[:, NBLK:SLOT, :].astype(F32)
    pieces = [small[pl.ds(r * 8, 8), b, :][None] for r in range(8) for b in range(6)]
    plain = swap_groups(jnp.concatenate(pieces, axis=0))
    for r in range(8):
        ks[r // 4, pl.ds(r % 4, NBLK, stride=BLK), :] = plain[r * 6 : r * 6 + 6].reshape(NBLK, DH)
    k = ks[0].astype(BF16)
    v = ks[1].astype(BF16)
    allowed = causal(col_ref[...], row_ref[...], 0)
    dk = jnp.zeros((QUART, DH), F32)
    dv = jnp.zeros((QUART, DH), F32)
    for n in range(GROUP):
        at = pl.ds(n * DH, DH)
        out, dq, dk_part, dv_part = attend(
            qs[n].astype(BF16), gs[n].astype(BF16), k, v, allowed
        )
        out_ref[:, at] = out
        dq_ref[:, at] = dq
        dk += dk_part
        dv += dv_part
    dk_ref[...] = dk.astype(BF16)
    dv_ref[...] = dv.astype(BF16)


def attend_tail(slots, seg_col, seg_row, partial):
    any_spec = pl.BlockSpec(memory_space=pl.ANY)
    last = lambda i: (3, 0)
    return pl.pallas_call(
        tail_kernel,
        grid=(1,),
        in_specs=[
            pl.BlockSpec((SEQ, SLOT, DH), lambda i: (0, 0, 0)),
            pl.BlockSpec((QUART, 1), last),
            pl.BlockSpec((1, QUART), lambda i: (0, 0)),
        ]
        + [any_spec] * 4,
        out_specs=[
            pl.BlockSpec((QUART, QW), last),
            pl.BlockSpec((QUART, QW), last),
            pl.BlockSpec((QUART, DH), last),
            pl.BlockSpec((QUART, DH), last),
        ],
        out_shape=OUT_SHAPES,
        input_output_aliases={3: 0, 4: 1, 5: 2, 6: 3},
        scratch_shapes=[
            pltpu.VMEM((GROUP, QUART, DH), F32),
            pltpu.VMEM((GROUP, QUART, DH), F32),
            pltpu.VMEM((2, QUART, DH), F32),
            pltpu.VMEM((SEQ, 8, DH), F32),
        ],
        compiler_params=params(),
        cost_estimate=pl.CostEstimate(
            flops=6 * 2 * GROUP * QUART * QUART * DH,
            bytes_accessed=2_000_000,
            transcendentals=GROUP * QUART * QUART,
        ),
        name="attend_tail",
    )(slots, seg_col, seg_row, *partial)


def on_device(queries, key_rows, value_rows, out_grad, mover_dest, segment_ids):
    me = lax.axis_index("head").astype(jnp.int32)
    held = (queries, key_rows, value_rows, out_grad)
    send = lambda x, *pairs: lax.ppermute(x, "head", list(pairs))
    plan_row = jnp.pad(mover_dest, (0, DH - NBLK)).reshape(1, DH)
    seg_col = segment_ids.reshape(ROWS, 1)
    seg_row = segment_ids.reshape(1, ROWS)

    one_lo, one_hi = pack_tail(*held, plan_row, 1)
    at_zero = send(one_lo, (3, 0))
    at_two = send(one_hi, (3, 2))
    to_zero = [send(x, (3, 0)) for x in pack_tail(*held, plan_row, 0)]
    to_two = [send(x, (3, 2)) for x in pack_tail(*held, plan_row, 2)]
    to_one = [send(at_zero, (0, 1)), send(at_two, (2, 1))]
    kept = pack_tail(*held, plan_row, 3)
    mine = []
    for half in range(2):
        other = jnp.where(me == 2, to_two[half], to_one[half])
        other = jnp.where(me == 0, to_zero[half], other)
        mine.append(jnp.where(me == 3, kept[half], other))
    slots = jnp.concatenate(mine, axis=0)

    pieces = lax.all_to_all(slots, "seq", split_axis=0, concat_axis=0, tiled=True)

    held_later = lax.optimization_barrier(held + (slots,))[:4]
    part = lambda shift: slice_group(*held_later, (me + shift) % 4)
    ahead, behind, across = part(1), part(3), part(2)
    relay = send(send(across, (1, 0)), (0, 3))
    plus = send(ahead, (0, 1), (1, 2), (2, 3))
    minus = send(behind, (1, 0), (2, 1), (0, 3))
    two = send(across, (0, 2), (2, 0))
    partial = attend_stay(me, held, (plus, minus, two, relay), seg_col, seg_row)

    routed = lax.all_to_all(route(pieces), "seq", split_axis=0, concat_axis=0, tiled=True)
    return attend_tail(routed, seg_col, seg_row[:, STAY:], partial)


def solution(mesh):
    rows = P(("seq", "head"), None)
    spread = P("seq", "head")
    return jax.shard_map(
        on_device,
        mesh=mesh,
        in_specs=(rows, rows, rows, rows, P("seq"), P("seq")),
        out_specs=(spread, spread, spread, spread),
        check_vma=False,
    )
```

```python
import math

import jax
import jax.numpy as jnp
from jax import lax
from jax.experimental import pallas as pl
from jax.experimental.pallas import tpu as pltpu
from jax.sharding import PartitionSpec as P

DH = 128
GROUP = 8
QW = GROUP * DH
ROWS = 768
QUART = 192
STAY = 576
BLK = 4
NBLK = 48
SEQ = 64
WIDE = 2 * QW + 2 * DH
FIRST = 16
REST = NBLK - FIRST
SLOT_A = FIRST + 8
SLOT = NBLK + 8
INV = 1.0 / math.sqrt(DH)
LOG2E = math.log2(math.e)
NEG = -1e30
F32 = jnp.float32
BF16 = jnp.bfloat16
VMEM_LIMIT = 56 * 1024 * 1024


def params():
    return pltpu.CompilerParams(vmem_limit_bytes=VMEM_LIMIT)


def cost(flops, bytes_accessed, transcendentals=0):
    return pl.CostEstimate(
        flops=flops, bytes_accessed=bytes_accessed, transcendentals=transcendentals
    )


def iota(shape, axis):
    return lax.broadcasted_iota(jnp.int32, shape, axis)


def swap_groups(x):
    sub = iota(x.shape, 1)
    grp = iota(x.shape, 2) // 16
    for bit in (1, 2, 4):
        s_on = (sub & bit) != 0
        l_on = (grp & bit) != 0
        up = pltpu.roll(pltpu.roll(x, 8 - bit, 1), 16 * bit, 2)
        down = pltpu.roll(pltpu.roll(x, bit, 1), 128 - 16 * bit, 2)
        x = jnp.where(s_on == l_on, x, jnp.where(l_on, up, down))
    return x


def split_rows(src, dst, first, count, qs):
    for n in range(GROUP):
        qs[n] = src[:, n * DH : (n + 1) * DH].astype(F32)
        for t in range(BLK):
            rows = qs[n, pl.ds(first * BLK + t, count, stride=BLK), :]
            dst[t * GROUP + n, 0:count, :] = rows.astype(BF16)


ORDER = (1, 0, 2, 3)


def pack_a_kernel(q_ref, k_ref, v_ref, g_ref, plan_ref, o1, o0, o2, o3, qs, ks, small):
    half = SEQ // 2
    plan = jnp.concatenate([plan_ref[...], jnp.zeros((1, DH - NBLK), jnp.int32)], axis=1)
    small[:, 6, :] = jnp.broadcast_to((plan // 64).astype(F32), (SEQ, DH))
    small[:, 7, :] = jnp.broadcast_to((plan % 64).astype(F32), (SEQ, DH))
    for group, out in zip(ORDER, (o1, o0, o2, o3)):
        thin = slice(group * DH, (group + 1) * DH)
        wide = slice(group * QW, (group + 1) * QW)
        ks[0] = k_ref[:, thin].astype(F32)
        ks[1] = v_ref[:, thin].astype(F32)
        pieces = []
        for r in range(8):
            rows = ks[r // 4, pl.ds(r % 4, NBLK, stride=BLK), :]
            pieces.append(rows.reshape(6, 8, DH))
        mixed = swap_groups(jnp.concatenate(pieces, axis=0))
        for r in range(8):
            for b in range(6):
                small[pl.ds(r * 8, 8), b, :] = mixed[r * 6 + b]
        for src, dst, start in ((q_ref, out.at[0:half], 0), (g_ref, out.at[half:SEQ], half)):
            split_rows(src.at[:, wide], dst, 0, FIRST, qs)
            dst[:, FIRST:SLOT_A, :] = small[pl.ds(start, half)].astype(BF16)


def pack_b_kernel(q_ref, g_ref, o1, o0, o2, o3, qs):
    half = SEQ // 2
    for group, out in zip(ORDER, (o1, o0, o2, o3)):
        wide = slice(group * QW, (group + 1) * QW)
        split_rows(q_ref.at[:, wide], out.at[0:half], FIRST, REST, qs)
        split_rows(g_ref.at[:, wide], out.at[half:SEQ], FIRST, REST, qs)


def packed_shapes(rows):
    return [jax.ShapeDtypeStruct((SEQ, rows, DH), BF16)] * 4


def pack_a(queries, key_rows, value_rows, out_grad, plan_row):
    shapes = packed_shapes(SLOT_A)
    top = lambda i: (0, 0)
    return pl.pallas_call(
        pack_a_kernel,
        grid=(1,),
        in_specs=[
            pl.BlockSpec((FIRST * BLK, 4 * QW), top),
            pl.BlockSpec((QUART, 4 * DH), top),
            pl.BlockSpec((QUART, 4 * DH), top),
            pl.BlockSpec((FIRST * BLK, 4 * QW), top),
            pl.BlockSpec((1, NBLK), top),
        ],
        out_specs=[pl.BlockSpec(x.shape, lambda i: (0, 0, 0)) for x in shapes],
        out_shape=shapes,
        scratch_shapes=[
            pltpu.VMEM((GROUP, FIRST * BLK, DH), F32),
            pltpu.VMEM((2, QUART, DH), F32),
            pltpu.VMEM((SEQ, 8, DH), F32),
        ],
        compiler_params=params(),
        cost_estimate=cost(0, 3_000_000),
        name="pack_a",
    )(queries, key_rows, value_rows, out_grad, plan_row)


def pack_b(queries, out_grad):
    shapes = packed_shapes(REST)
    return pl.pallas_call(
        pack_b_kernel,
        grid=(1,),
        in_specs=[pl.BlockSpec((QUART, 4 * QW), lambda i: (0, 0))] * 2,
        out_specs=[pl.BlockSpec(x.shape, lambda i: (0, 0, 0)) for x in shapes],
        out_shape=shapes,
        scratch_shapes=[pltpu.VMEM((GROUP, QUART, DH), F32)],
        compiler_params=params(),
        cost_estimate=cost(0, 5_000_000),
        name="pack_b",
    )(queries, out_grad)


def slice_kernel(me_ref, q_ref, k_ref, v_ref, g_ref, o_ref):
    o_ref[:, 0:QW] = q_ref[...]
    o_ref[:, QW : 2 * QW] = g_ref[...]
    o_ref[:, 2 * QW : 2 * QW + DH] = k_ref[...]
    o_ref[:, 2 * QW + DH : WIDE] = v_ref[...]


def slice_group(queries, key_rows, value_rows, out_grad, group):
    column = lambda i, g: (0, g[0])
    return pl.pallas_call(
        slice_kernel,
        grid_spec=pltpu.PrefetchScalarGridSpec(
            num_scalar_prefetch=1,
            grid=(1,),
            in_specs=[
                pl.BlockSpec((QUART, QW), column),
                pl.BlockSpec((QUART, DH), column),
                pl.BlockSpec((QUART, DH), column),
                pl.BlockSpec((QUART, QW), column),
            ],
            out_specs=pl.BlockSpec((QUART, WIDE), lambda i, g: (0, 0)),
        ),
        out_shape=jax.ShapeDtypeStruct((QUART, WIDE), BF16),
        compiler_params=params(),
        cost_estimate=cost(0, 1_800_000),
        name="slice_group",
    )(group.reshape(1), queries, key_rows, value_rows, out_grad)


def plan_lines(tail, first, count):
    total = SEQ * count
    col = iota((1, total), 1).astype(F32)
    owner = jnp.floor((col + 0.5) * (1.0 / count))
    place = col - owner * count + first
    pick = (iota((DH, total), 0).astype(F32) == place).astype(BF16)
    mine = iota((SEQ, total), 0).astype(F32) == owner
    lines = []
    for row in (6, 7):
        spread = jnp.dot(tail[:, row, :].astype(BF16), pick, preferred_element_type=F32)
        lines.append(jnp.sum(jnp.where(mine, spread, 0.0), axis=0, keepdims=True))
    return lines


def low_choice(line):
    return (iota((64, line.shape[1]), 0).astype(F32) == line).astype(BF16)


def choose(sel, low, line, first, runs):
    for k in range(runs):
        row = jnp.where(line == float(first + k), 1.0, 0.0).astype(BF16)
        sel[k * 64 : (k + 1) * 64, :] = low * row


PARTS = 4
TILE = SEQ * NBLK // PARTS
RUNS = TILE // 64
SHARDS = TILE // NBLK


def merge(got, here, shard, out_ref, part_ref=None):
    out = got[:, 0:DH].astype(BF16)
    kept = jnp.where(here, got[:, DH : 2 * DH], 0.0)
    sums = [jnp.sum(kept[b * 8 : b * 8 + 8], axis=0, keepdims=True) for b in range(6)]
    packed = jnp.concatenate(sums + [jnp.zeros((2, DH), F32)], axis=0).astype(BF16)
    if part_ref is not None:
        out += part_ref[shard, 0:NBLK, :]
        packed += part_ref[shard, NBLK:SLOT, :]
    out_ref[shard, 0:NBLK, :] = out
    out_ref[shard, NBLK:SLOT, :] = packed


def lane_is_row():
    return iota((NBLK, DH), 1) // 16 == iota((NBLK, DH), 0) % 8


def route_a_kernel(in_ref, out_ref, line_ref, low_ref, rest_ref, xs, ks, sel, low_a):
    tail = in_ref[:, FIRST:SLOT_A, :].astype(F32)
    high_a, digits_a = plan_lines(tail, 0, FIRST)
    high_b, digits_b = plan_lines(tail, FIRST, REST)
    line_ref[...] = jnp.broadcast_to(high_b, line_ref.shape)
    low_ref[...] = low_choice(digits_b)
    low_a[...] = low_choice(digits_a)

    here = lane_is_row()
    fold = (iota((DH, DH), 0) % 16 == iota((DH, DH), 1) % 16).astype(BF16)
    for s in range(SEQ):
        xs[s * FIRST : (s + 1) * FIRST, 0:DH] = in_ref[s, 0:FIRST, :]
        rows = [jnp.broadcast_to(tail[s, b : b + 1, :], (8, DH)) for b in range(6)]
        wide = jnp.where(here, jnp.concatenate(rows, axis=0), 0.0).astype(BF16)
        ks[s * FIRST : (s + 1) * FIRST, :] = wide[0:FIRST]
        rest_ref[s * REST : (s + 1) * REST, :] = wide[FIRST:NBLK]
    xs[:, DH : 2 * DH] = jnp.dot(ks[...], fold, preferred_element_type=F32).astype(BF16)
    rest_ref[...] = jnp.dot(rest_ref[...], fold, preferred_element_type=F32).astype(BF16)
    for p in range(PARTS):
        choose(sel.at[p % 2], low_a[...], high_a, p * RUNS, RUNS)
        got = jnp.dot(sel[p % 2], xs[...], preferred_element_type=F32)
        for d in range(SHARDS):
            merge(got[d * NBLK : (d + 1) * NBLK], here, p * SHARDS + d, out_ref)


def route_a(slots):
    vmem = pl.BlockSpec(memory_space=pltpu.VMEM)
    return pl.pallas_call(
        route_a_kernel,
        in_specs=[vmem],
        out_specs=[vmem] * 4,
        out_shape=[
            jax.ShapeDtypeStruct((SEQ, SLOT, DH), BF16),
            jax.ShapeDtypeStruct((8, SEQ * REST), F32),
            jax.ShapeDtypeStruct((64, SEQ * REST), BF16),
            jax.ShapeDtypeStruct((SEQ * REST, DH), BF16),
        ],
        scratch_shapes=[
            pltpu.VMEM((SEQ * FIRST, 2 * DH), BF16),
            pltpu.VMEM((SEQ * FIRST, DH), BF16),
            pltpu.VMEM((2, TILE, SEQ * FIRST), BF16),
            pltpu.VMEM((64, SEQ * FIRST), BF16),
        ],
        compiler_params=params(),
        cost_estimate=cost(4 * SEQ * NBLK * SEQ * FIRST * DH, 2_000_000),
        name="route_a",
    )(slots)


def route_b_kernel(in_ref, part_ref, line_ref, low_ref, rest_ref, out_ref, xs, sel):
    xs[:, 0:DH] = in_ref[...].reshape(SEQ * REST, DH)
    xs[:, DH : 2 * DH] = rest_ref[...]
    here = lane_is_row()
    line = line_ref[0:1, :]
    for p in range(PARTS):
        choose(sel.at[p % 2], low_ref[...], line, p * RUNS, RUNS)
        got = jnp.dot(sel[p % 2], xs[...], preferred_element_type=F32)
        for d in range(SHARDS):
            merge(got[d * NBLK : (d + 1) * NBLK], here, p * SHARDS + d, out_ref, part_ref)


def route_b(slots, part, line, low, rest):
    vmem = pl.BlockSpec(memory_space=pltpu.VMEM)
    return pl.pallas_call(
        route_b_kernel,
        in_specs=[vmem] * 5,
        out_specs=vmem,
        out_shape=jax.ShapeDtypeStruct((SEQ, SLOT, DH), BF16),
        scratch_shapes=[
            pltpu.VMEM((SEQ * REST, 2 * DH), BF16),
            pltpu.VMEM((2, TILE, SEQ * REST), BF16),
        ],
        compiler_params=params(),
        cost_estimate=cost(4 * SEQ * NBLK * SEQ * REST * DH, 3_000_000),
        name="route_b",
    )(slots, part, line, low, rest)


def dot(a, b, dims):
    return lax.dot_general(a, b, (dims, ((), ())), preferred_element_type=F32)


NT = ((1,), (1,))
NN = ((1,), (0,))


def attend(q, g, k, v, k_cols, v_cols, allowed):
    scores = jnp.where(allowed, dot(k, q, NT) * (INV * LOG2E), NEG)
    weights = jnp.exp2(scores - jnp.max(scores, axis=0, keepdims=True))
    probs = weights * (1.0 / jnp.sum(weights, axis=0, keepdims=True))
    probs_low = probs.astype(BF16)
    grad_probs = dot(v, g, NT)
    centre = jnp.sum(probs * grad_probs, axis=0, keepdims=True)
    grad_scores = (probs * (grad_probs - centre) * INV).astype(BF16)
    out_cols = dot(v_cols, probs_low, NN)
    dq_cols = dot(k_cols, grad_scores, NN)
    return out_cols, dq_cols, dot(grad_scores, q, NN), dot(probs_low, g, NN)


def causal(seg_col, seg_row, first):
    j = iota((seg_col.shape[0], DH), 0)
    i = iota((seg_col.shape[0], DH), 1) + first
    return (seg_col == seg_row) & (j <= i)


PAD = 640
PAIR = 2


def stay_kernel(
    me_ref, q_any, k_any, v_any, g_any, plus, minus, two, col_ref, row_ref,
    out_ref, dq_ref, dk_ref, dv_ref, rows, kt, vt, dk, dv, sems,
):
    me = me_ref[0]

    def fetch(src, part):
        pltpu.make_async_copy(src, rows.at[pl.ds(part * QUART, QUART), :], sems.at[part]).start()

    wide = pl.ds(pl.multiple_of(me * QW, QW), QW)
    thin = pl.ds(pl.multiple_of(me * DH, DH), DH)

    def own(part):
        there = pl.ds(part * QUART, QUART)
        columns = (0, QW, 2 * QW, 2 * QW + DH, WIDE)
        for n, (src, at) in enumerate(((q_any, wide), (g_any, wide), (k_any, thin), (v_any, thin))):
            pltpu.make_async_copy(
                src.at[:, at], rows.at[there, columns[n] : columns[n + 1]], sems.at[part]
            ).start()

    @pl.when(me == 0)
    def _():
        own(0)
        fetch(minus, 1)
        fetch(two, 2)

    @pl.when(me == 1)
    def _():
        fetch(plus, 0)
        own(1)
        fetch(minus, 2)

    @pl.when(me == 2)
    def _():
        fetch(two, 0)
        fetch(plus, 1)
        own(2)

    @pl.when(me == 3)
    def _():
        fetch(minus, 0)
        fetch(two, 1)
        fetch(plus, 2)

    dk[...] = jnp.zeros_like(dk)
    dv[...] = jnp.zeros_like(dv)
    rows[STAY:PAD, :] = jnp.zeros((PAD - STAY, WIDE), BF16)
    for part in range(3):
        pltpu.make_async_copy(plus, rows.at[pl.ds(part * QUART, QUART), :], sems.at[part]).wait()
    kt[...] = rows[:, 2 * QW : 2 * QW + DH].astype(F32).T.astype(BF16)
    vt[...] = rows[:, 2 * QW + DH : WIDE].astype(F32).T.astype(BF16)

    for tile in range(PAD // DH):
        width = (tile + 1) * DH
        there = slice(tile * DH, width)
        count = min(DH, STAY - tile * DH)
        allowed = causal(col_ref[0:width, :], row_ref[:, there], tile * DH)
        allowed = jnp.concatenate([allowed] * PAIR, axis=1)

        for first in range(0, GROUP, PAIR):
            heads = range(first, first + PAIR)
            q = [rows[there, n * DH : (n + 1) * DH] for n in heads]
            g = [rows[there, QW + n * DH : QW + (n + 1) * DH] for n in heads]
            out, dq, dk_part, dv_part = attend(
                jnp.concatenate(q, axis=0),
                jnp.concatenate(g, axis=0),
                rows[0:width, 2 * QW : 2 * QW + DH],
                rows[0:width, 2 * QW + DH : WIDE],
                kt[:, 0:width],
                vt[:, 0:width],
                allowed,
            )
            for h, n in enumerate(heads):
                at = slice(n * DH, (n + 1) * DH)
                columns = slice(h * DH, (h + 1) * DH)
                out_ref[tile * DH : tile * DH + count, at] = out[:, columns].T[0:count].astype(BF16)
                dq_ref[tile * DH : tile * DH + count, at] = dq[:, columns].T[0:count].astype(BF16)
            dk[0:width, :] += dk_part
            dv[0:width, :] += dv_part

    dk_ref[...] = dk[0:STAY, :].astype(BF16)
    dv_ref[...] = dv[0:STAY, :].astype(BF16)


OUT_SHAPES = [
    jax.ShapeDtypeStruct((ROWS, QW), BF16),
    jax.ShapeDtypeStruct((ROWS, QW), BF16),
    jax.ShapeDtypeStruct((ROWS, DH), BF16),
    jax.ShapeDtypeStruct((ROWS, DH), BF16),
]


def attend_stay(me, held, received, seg_col, seg_row):
    any_spec = pl.BlockSpec(memory_space=pl.ANY)
    top = lambda n, m: (0, 0)
    return pl.pallas_call(
        stay_kernel,
        grid_spec=pltpu.PrefetchScalarGridSpec(
            num_scalar_prefetch=1,
            grid=(1,),
            in_specs=[any_spec] * 7 + [pl.BlockSpec((ROWS, 1), top), pl.BlockSpec((1, ROWS), top)],
            out_specs=[
                pl.BlockSpec((STAY, QW), top),
                pl.BlockSpec((STAY, QW), top),
                pl.BlockSpec((STAY, DH), top),
                pl.BlockSpec((STAY, DH), top),
            ],
            scratch_shapes=[
                pltpu.VMEM((PAD, WIDE), BF16),
                pltpu.VMEM((DH, PAD), BF16),
                pltpu.VMEM((DH, PAD), BF16),
                pltpu.VMEM((PAD, DH), F32),
                pltpu.VMEM((PAD, DH), F32),
                pltpu.SemaphoreType.DMA((3,)),
            ],
        ),
        out_shape=OUT_SHAPES,
        compiler_params=params(),
        cost_estimate=cost(60 * 2 * GROUP * STAY * STAY * DH, 6_000_000, GROUP * STAY * STAY),
        name="attend_stay",
    )(me.reshape(1), *held, *received, seg_col, seg_row)


SPAN = 2 * DH


def tail_kernel(
    slots, col_ref, row_ref, a0, a1, a2, a3, out_ref, dq_ref, dk_ref, dv_ref, qs, gs, ks, small
):
    pad = jnp.zeros((SPAN - QUART, DH), F32)
    for n in range(GROUP):
        qs[n, QUART:SPAN, :] = pad
        gs[n, QUART:SPAN, :] = pad
        for t in range(BLK):
            there = pl.ds(t, NBLK, stride=BLK)
            qs[n, there, :] = slots[t * GROUP + n, 0:NBLK, :].astype(F32)
            gs[n, there, :] = slots[SEQ // 2 + t * GROUP + n, 0:NBLK, :].astype(F32)
    small[...] = slots[:, NBLK:SLOT, :].astype(F32)
    pieces = [small[pl.ds(r * 8, 8), b, :][None] for r in range(8) for b in range(6)]
    plain = swap_groups(jnp.concatenate(pieces, axis=0))
    for r in range(8):
        ks[r // 4, pl.ds(r % 4, NBLK, stride=BLK), :] = plain[r * 6 : r * 6 + 6].reshape(NBLK, DH)
    for half in range(2):
        ks[half, QUART:SPAN, :] = pad
    for tile in range(2):
        first = tile * DH
        count = min(DH, QUART - first)
        there = slice(first, first + DH)
        k, v = ks[0, there, :], ks[1, there, :]
        allowed = causal(col_ref[there, :], row_ref[:, there], 0)
        out, dq, dk, dv = attend(
            qs[:, there, :].astype(BF16).reshape(QW, DH),
            gs[:, there, :].astype(BF16).reshape(QW, DH),
            k.astype(BF16),
            v.astype(BF16),
            k.T.astype(BF16),
            v.T.astype(BF16),
            jnp.concatenate([allowed] * GROUP, axis=1),
        )
        for n in range(GROUP):
            at = slice(n * DH, (n + 1) * DH)
            out_ref[first : first + count, at] = out[:, at].T[0:count].astype(BF16)
            dq_ref[first : first + count, at] = dq[:, at].T[0:count].astype(BF16)
        dk_ref[first : first + count, :] = dk[0:count].astype(BF16)
        dv_ref[first : first + count, :] = dv[0:count].astype(BF16)


def attend_tail(slots, seg_col, seg_row, partial):
    any_spec = pl.BlockSpec(memory_space=pl.ANY)
    last = lambda i: (3, 0)
    return pl.pallas_call(
        tail_kernel,
        grid=(1,),
        in_specs=[
            pl.BlockSpec((SEQ, SLOT, DH), lambda i: (0, 0, 0)),
            pl.BlockSpec((SPAN, 1), lambda i: (0, 0)),
            pl.BlockSpec((1, SPAN), lambda i: (0, 0)),
        ]
        + [any_spec] * 4,
        out_specs=[
            pl.BlockSpec((QUART, QW), last),
            pl.BlockSpec((QUART, QW), last),
            pl.BlockSpec((QUART, DH), last),
            pl.BlockSpec((QUART, DH), last),
        ],
        out_shape=OUT_SHAPES,
        input_output_aliases={3: 0, 4: 1, 5: 2, 6: 3},
        scratch_shapes=[
            pltpu.VMEM((GROUP, SPAN, DH), F32),
            pltpu.VMEM((GROUP, SPAN, DH), F32),
            pltpu.VMEM((2, SPAN, DH), F32),
            pltpu.VMEM((SEQ, 8, DH), F32),
        ],
        compiler_params=params(),
        cost_estimate=cost(6 * 2 * GROUP * QUART * DH * DH, 2_000_000, GROUP * QUART * DH),
        name="attend_tail",
    )(slots, seg_col, seg_row, *partial)


def after(values, *others):
    return lax.optimization_barrier((tuple(values), others))[0]


def on_device(queries, key_rows, value_rows, out_grad, mover_dest, segment_ids):
    me = lax.axis_index("head").astype(jnp.int32)
    held = (queries, key_rows, value_rows, out_grad)
    send = lambda x, *pairs: lax.ppermute(x, "head", list(pairs))
    exchange = lambda x: lax.all_to_all(x, "seq", split_axis=0, concat_axis=0, tiled=True)

    def scatter(one, zero, two, three):
        parts = (send(one, (3, 1)), send(zero, (3, 0)), send(two, (3, 2)))
        other = jnp.where(me == 0, parts[1], jnp.where(me == 2, parts[2], parts[0]))
        return jnp.where(me == 3, three, other), parts

    slots_a, sent_a = scatter(*pack_a(*held, mover_dest.reshape(1, NBLK)))
    part = lambda shift: slice_group(*held, (me + shift) % 4)
    slices = (part(1), part(3), part(2))
    slots_b, _ = scatter(*after(pack_b(queries, out_grad), *sent_a, *slices))

    pieces_a = exchange(slots_a)
    (next_b,) = after([slots_b], pieces_a)
    pieces_b = exchange(next_b)
    routed_a = route_a(pieces_a)

    ahead, behind, across = after(slices, slots_b)
    two = send(across, (0, 2), (2, 0), (1, 3))
    plus = send(ahead, (0, 1), (1, 2), (2, 3))
    minus = send(behind, (1, 0), (2, 1), (0, 3))

    routed = route_b(pieces_b, *routed_a)
    stay = after((plus, minus, two), routed)
    seg_col = segment_ids.reshape(ROWS, 1)
    seg_row = segment_ids.reshape(1, ROWS)
    tail_seg = jnp.pad(segment_ids[STAY:], (0, SPAN - QUART), constant_values=-1)
    partial = attend_stay(me, held, stay, seg_col, seg_row)
    arrived = exchange(routed)
    return attend_tail(arrived, tail_seg.reshape(SPAN, 1), tail_seg.reshape(1, SPAN), partial)


def solution(mesh):
    rows = P(("seq", "head"), None)
    spread = P("seq", "head")
    return jax.shard_map(
        on_device,
        mesh=mesh,
        in_specs=(rows, rows, rows, rows, P("seq"), P("seq")),
        out_specs=(spread, spread, spread, spread),
        check_vma=False,
    )
```

```python
import math

import jax
import jax.numpy as jnp
from jax import lax
from jax.experimental import pallas as pl
from jax.experimental.pallas import tpu as pltpu
from jax.sharding import PartitionSpec as P

DH = 128
GROUP = 8
QW = GROUP * DH
ROWS = 768
QUART = 192
STAY = 576
BLK = 4
NBLK = 48
SEQ = 64
WIDE = 2 * QW + 2 * DH
SLOT = NBLK + 8
INV = 1.0 / math.sqrt(DH)
LOG2E = math.log2(math.e)
NEG = -1e30
F32 = jnp.float32
BF16 = jnp.bfloat16
VMEM_LIMIT = 56 * 1024 * 1024


def params():
    return pltpu.CompilerParams(vmem_limit_bytes=VMEM_LIMIT)


def cost(flops, bytes_accessed, transcendentals=0):
    return pl.CostEstimate(
        flops=flops, bytes_accessed=bytes_accessed, transcendentals=transcendentals
    )


def iota(shape, axis):
    return lax.broadcasted_iota(jnp.int32, shape, axis)


def swap_groups(x):
    sub = iota(x.shape, 1)
    grp = iota(x.shape, 2) // 16
    for bit in (1, 2, 4):
        s_on = (sub & bit) != 0
        l_on = (grp & bit) != 0
        up = pltpu.roll(pltpu.roll(x, 8 - bit, 1), 16 * bit, 2)
        down = pltpu.roll(pltpu.roll(x, bit, 1), 128 - 16 * bit, 2)
        x = jnp.where(s_on == l_on, x, jnp.where(l_on, up, down))
    return x


def pack_group(group, q_ref, k_ref, v_ref, g_ref, out, qs, ks, small):
    half = SEQ // 2
    thin = slice(group * DH, (group + 1) * DH)
    ks[0] = k_ref[:, thin].astype(F32)
    ks[1] = v_ref[:, thin].astype(F32)
    pieces = []
    for r in range(8):
        rows = ks[r // 4, pl.ds(r % 4, NBLK, stride=BLK), :]
        pieces.append(rows.reshape(6, 8, DH))
    mixed = swap_groups(jnp.concatenate(pieces, axis=0))
    for r in range(8):
        for b in range(6):
            small[pl.ds(r * 8, 8), b, :] = mixed[r * 6 + b]
    for which, src in enumerate((q_ref, g_ref)):
        dst = out[which]
        for n in range(GROUP):
            qs[n] = src[:, group * QW + n * DH : group * QW + (n + 1) * DH].astype(F32)
            for t in range(BLK):
                rows = qs[n, pl.ds(t, NBLK, stride=BLK), :]
                dst[t * GROUP + n, 0:NBLK, :] = rows.astype(BF16)
        dst[:, NBLK:SLOT, :] = small[pl.ds(which * half, half)].astype(BF16)


def put_plan(plan_ref, small):
    plan = jnp.concatenate([plan_ref[...], jnp.zeros((1, DH - NBLK), jnp.int32)], axis=1)
    small[:, 6, :] = jnp.broadcast_to((plan // 64).astype(F32), (SEQ, DH))
    small[:, 7, :] = jnp.broadcast_to((plan % 64).astype(F32), (SEQ, DH))


def pack_one_kernel(q_ref, k_ref, v_ref, g_ref, plan_ref, lo_ref, hi_ref, qs, ks, small):
    put_plan(plan_ref, small)
    pack_group(0, q_ref, k_ref, v_ref, g_ref, (lo_ref, hi_ref), qs, ks, small)


def pack_rest_kernel(q_ref, k_ref, v_ref, g_ref, plan_ref, o0, o2, o3, qs, ks, small):
    half = SEQ // 2
    put_plan(plan_ref, small)
    for group, out in ((0, o0), (2, o2), (3, o3)):
        halves = (out.at[0:half], out.at[half:SEQ])
        pack_group(group, q_ref, k_ref, v_ref, g_ref, halves, qs, ks, small)


def pack(kernel, name, width, first, shapes, queries, key_rows, value_rows, out_grad, plan_row):
    at = lambda i: (0, first)
    return pl.pallas_call(
        kernel,
        grid=(1,),
        in_specs=[
            pl.BlockSpec((QUART, width * QW), at),
            pl.BlockSpec((QUART, width * DH), at),
            pl.BlockSpec((QUART, width * DH), at),
            pl.BlockSpec((QUART, width * QW), at),
            pl.BlockSpec((1, NBLK), lambda i: (0, 0)),
        ],
        out_specs=[pl.BlockSpec(x, lambda i: (0, 0, 0)) for x in shapes],
        out_shape=[jax.ShapeDtypeStruct(x, BF16) for x in shapes],
        scratch_shapes=[
            pltpu.VMEM((GROUP, QUART, DH), F32),
            pltpu.VMEM((2, QUART, DH), F32),
            pltpu.VMEM((SEQ, 8, DH), F32),
        ],
        compiler_params=params(),
        cost_estimate=cost(0, 2_000_000 * len(shapes)),
        name=name,
    )(queries, key_rows, value_rows, out_grad, plan_row)


def slice_kernel(me_ref, q_ref, k_ref, v_ref, g_ref, o_ref):
    o_ref[:, 0:QW] = q_ref[...]
    o_ref[:, QW : 2 * QW] = g_ref[...]
    o_ref[:, 2 * QW : 2 * QW + DH] = k_ref[...]
    o_ref[:, 2 * QW + DH : WIDE] = v_ref[...]


def slice_group(queries, key_rows, value_rows, out_grad, group):
    column = lambda i, g: (0, g[0])
    return pl.pallas_call(
        slice_kernel,
        grid_spec=pltpu.PrefetchScalarGridSpec(
            num_scalar_prefetch=1,
            grid=(1,),
            in_specs=[
                pl.BlockSpec((QUART, QW), column),
                pl.BlockSpec((QUART, DH), column),
                pl.BlockSpec((QUART, DH), column),
                pl.BlockSpec((QUART, QW), column),
            ],
            out_specs=pl.BlockSpec((QUART, WIDE), lambda i, g: (0, 0)),
        ),
        out_shape=jax.ShapeDtypeStruct((QUART, WIDE), BF16),
        compiler_params=params(),
        cost_estimate=cost(0, 1_800_000),
        name="slice_group",
    )(group.reshape(1), queries, key_rows, value_rows, out_grad)


def plan_lines(tail):
    total = SEQ * NBLK
    col = iota((1, total), 1).astype(F32)
    owner = jnp.floor((col + 0.5) * (1.0 / NBLK))
    place = col - owner * NBLK
    pick = (iota((DH, total), 0).astype(F32) == place).astype(BF16)
    mine = iota((SEQ, total), 0).astype(F32) == owner
    lines = []
    for row in (6, 7):
        spread = jnp.dot(tail[:, row, :].astype(BF16), pick, preferred_element_type=F32)
        lines.append(jnp.sum(jnp.where(mine, spread, 0.0), axis=0, keepdims=True))
    return lines


def low_choice(line):
    return (iota((64, line.shape[1]), 0).astype(F32) == line).astype(BF16)


def choose(sel, low, line, first, runs):
    for k in range(runs):
        row = jnp.where(line == float(first + k), 1.0, 0.0).astype(BF16)
        sel[k * 64 : (k + 1) * 64, :] = low * row


PARTS = 4
TILE = SEQ * NBLK // PARTS
RUNS = TILE // 64
SHARDS = TILE // NBLK


def route_kernel(in_ref, out_ref, xs, ks, sel, low):
    tail = in_ref[:, NBLK:SLOT, :].astype(F32)
    high, digits = plan_lines(tail)
    low[...] = low_choice(digits)
    here = iota((NBLK, DH), 1) // 16 == iota((NBLK, DH), 0) % 8
    fold = (iota((DH, DH), 0) % 16 == iota((DH, DH), 1) % 16).astype(BF16)
    xs[:, 0:DH] = in_ref[:, 0:NBLK, :].reshape(SEQ * NBLK, DH)
    for s in range(SEQ):
        rows = [jnp.broadcast_to(tail[s, b : b + 1, :], (8, DH)) for b in range(6)]
        wide = jnp.where(here, jnp.concatenate(rows, axis=0), 0.0).astype(BF16)
        ks[s * NBLK : (s + 1) * NBLK, :] = wide
    xs[:, DH : 2 * DH] = jnp.dot(ks[...], fold, preferred_element_type=F32).astype(BF16)
    for p in range(PARTS):
        choose(sel.at[p % 2], low[...], high, p * RUNS, RUNS)
        got = jnp.dot(sel[p % 2], xs[...], preferred_element_type=F32)
        for d in range(SHARDS):
            part = got[d * NBLK : (d + 1) * NBLK]
            kept = jnp.where(here, part[:, DH : 2 * DH], 0.0)
            sums = [jnp.sum(kept[b * 8 : b * 8 + 8], axis=0, keepdims=True) for b in range(6)]
            sums.append(jnp.zeros((2, DH), F32))
            out_ref[p * SHARDS + d, 0:NBLK, :] = part[:, 0:DH].astype(BF16)
            out_ref[p * SHARDS + d, NBLK:SLOT, :] = jnp.concatenate(sums, axis=0).astype(BF16)


def route(slots):
    vmem = pl.BlockSpec(memory_space=pltpu.VMEM)
    return pl.pallas_call(
        route_kernel,
        in_specs=[vmem],
        out_specs=vmem,
        out_shape=jax.ShapeDtypeStruct((SEQ, SLOT, DH), BF16),
        scratch_shapes=[
            pltpu.VMEM((SEQ * NBLK, 2 * DH), BF16),
            pltpu.VMEM((SEQ * NBLK, DH), BF16),
            pltpu.VMEM((2, TILE, SEQ * NBLK), BF16),
            pltpu.VMEM((64, SEQ * NBLK), BF16),
        ],
        compiler_params=params(),
        cost_estimate=cost(4 * SEQ * NBLK * SEQ * NBLK * DH, 2_000_000),
        name="route",
    )(slots)


def dot(a, b, dims):
    return lax.dot_general(a, b, (dims, ((), ())), preferred_element_type=F32)


NT = ((1,), (1,))
NN = ((1,), (0,))


def attend(q, g, k, v, k_cols, v_cols, allowed):
    scores = jnp.where(allowed, dot(k, q, NT) * (INV * LOG2E), NEG)
    weights = jnp.exp2(scores - jnp.max(scores, axis=0, keepdims=True))
    probs = weights * (1.0 / jnp.sum(weights, axis=0, keepdims=True))
    probs_low = probs.astype(BF16)
    grad_probs = dot(v, g, NT)
    centre = jnp.sum(probs * grad_probs, axis=0, keepdims=True)
    grad_scores = (probs * (grad_probs - centre) * INV).astype(BF16)
    out_cols = dot(v_cols, probs_low, NN)
    dq_cols = dot(k_cols, grad_scores, NN)
    return out_cols, dq_cols, dot(grad_scores, q, NN), dot(probs_low, g, NN)


def causal(seg_col, seg_row, first):
    j = iota((seg_col.shape[0], DH), 0)
    i = iota((seg_col.shape[0], DH), 1) + first
    return (seg_col == seg_row) & (j <= i)


PAD = 640
PAIR = 2


def stay_kernel(
    me_ref, q_any, k_any, v_any, g_any, plus, minus, two, col_ref, row_ref,
    out_ref, dq_ref, dk_ref, dv_ref, rows, kt, vt, dk, dv, sems,
):
    me = me_ref[0]

    def fetch(src, part):
        pltpu.make_async_copy(src, rows.at[pl.ds(part * QUART, QUART), :], sems.at[part]).start()

    wide = pl.ds(pl.multiple_of(me * QW, QW), QW)
    thin = pl.ds(pl.multiple_of(me * DH, DH), DH)

    def own(part):
        there = pl.ds(part * QUART, QUART)
        columns = (0, QW, 2 * QW, 2 * QW + DH, WIDE)
        for n, (src, at) in enumerate(((q_any, wide), (g_any, wide), (k_any, thin), (v_any, thin))):
            pltpu.make_async_copy(
                src.at[:, at], rows.at[there, columns[n] : columns[n + 1]], sems.at[part]
            ).start()

    @pl.when(me == 0)
    def _():
        own(0)
        fetch(minus, 1)
        fetch(two, 2)

    @pl.when(me == 1)
    def _():
        fetch(plus, 0)
        own(1)
        fetch(minus, 2)

    @pl.when(me == 2)
    def _():
        fetch(two, 0)
        fetch(plus, 1)
        own(2)

    @pl.when(me == 3)
    def _():
        fetch(minus, 0)
        fetch(two, 1)
        fetch(plus, 2)

    dk[...] = jnp.zeros_like(dk)
    dv[...] = jnp.zeros_like(dv)
    rows[STAY:PAD, :] = jnp.zeros((PAD - STAY, WIDE), BF16)
    for part in range(3):
        pltpu.make_async_copy(plus, rows.at[pl.ds(part * QUART, QUART), :], sems.at[part]).wait()
    kt[...] = rows[:, 2 * QW : 2 * QW + DH].astype(F32).T.astype(BF16)
    vt[...] = rows[:, 2 * QW + DH : WIDE].astype(F32).T.astype(BF16)

    for tile in range(PAD // DH):
        width = (tile + 1) * DH
        there = slice(tile * DH, width)
        count = min(DH, STAY - tile * DH)
        allowed = causal(col_ref[0:width, :], row_ref[:, there], tile * DH)
        allowed = jnp.concatenate([allowed] * PAIR, axis=1)

        for first in range(0, GROUP, PAIR):
            heads = range(first, first + PAIR)
            q = [rows[there, n * DH : (n + 1) * DH] for n in heads]
            g = [rows[there, QW + n * DH : QW + (n + 1) * DH] for n in heads]
            out, dq, dk_part, dv_part = attend(
                jnp.concatenate(q, axis=0),
                jnp.concatenate(g, axis=0),
                rows[0:width, 2 * QW : 2 * QW + DH],
                rows[0:width, 2 * QW + DH : WIDE],
                kt[:, 0:width],
                vt[:, 0:width],
                allowed,
            )
            for h, n in enumerate(heads):
                at = slice(n * DH, (n + 1) * DH)
                columns = slice(h * DH, (h + 1) * DH)
                out_ref[tile * DH : tile * DH + count, at] = out[:, columns].T[0:count].astype(BF16)
                dq_ref[tile * DH : tile * DH + count, at] = dq[:, columns].T[0:count].astype(BF16)
            dk[0:width, :] += dk_part
            dv[0:width, :] += dv_part

    dk_ref[...] = dk[0:STAY, :].astype(BF16)
    dv_ref[...] = dv[0:STAY, :].astype(BF16)


OUT_SHAPES = [
    jax.ShapeDtypeStruct((ROWS, QW), BF16),
    jax.ShapeDtypeStruct((ROWS, QW), BF16),
    jax.ShapeDtypeStruct((ROWS, DH), BF16),
    jax.ShapeDtypeStruct((ROWS, DH), BF16),
]


def attend_stay(me, held, received, seg_col, seg_row):
    any_spec = pl.BlockSpec(memory_space=pl.ANY)
    top = lambda n, m: (0, 0)
    return pl.pallas_call(
        stay_kernel,
        grid_spec=pltpu.PrefetchScalarGridSpec(
            num_scalar_prefetch=1,
            grid=(1,),
            in_specs=[any_spec] * 7 + [pl.BlockSpec((ROWS, 1), top), pl.BlockSpec((1, ROWS), top)],
            out_specs=[
                pl.BlockSpec((STAY, QW), top),
                pl.BlockSpec((STAY, QW), top),
                pl.BlockSpec((STAY, DH), top),
                pl.BlockSpec((STAY, DH), top),
            ],
            scratch_shapes=[
                pltpu.VMEM((PAD, WIDE), BF16),
                pltpu.VMEM((DH, PAD), BF16),
                pltpu.VMEM((DH, PAD), BF16),
                pltpu.VMEM((PAD, DH), F32),
                pltpu.VMEM((PAD, DH), F32),
                pltpu.SemaphoreType.DMA((3,)),
            ],
        ),
        out_shape=OUT_SHAPES,
        compiler_params=params(),
        cost_estimate=cost(60 * 2 * GROUP * STAY * STAY * DH, 6_000_000, GROUP * STAY * STAY),
        name="attend_stay",
    )(me.reshape(1), *held, *received, seg_col, seg_row)


SPAN = 2 * DH


def tail_kernel(
    slots, col_ref, row_ref, a0, a1, a2, a3, out_ref, dq_ref, dk_ref, dv_ref, qs, gs, ks, small
):
    pad = jnp.zeros((SPAN - QUART, DH), F32)
    for n in range(GROUP):
        qs[n, QUART:SPAN, :] = pad
        gs[n, QUART:SPAN, :] = pad
        for t in range(BLK):
            there = pl.ds(t, NBLK, stride=BLK)
            qs[n, there, :] = slots[t * GROUP + n, 0:NBLK, :].astype(F32)
            gs[n, there, :] = slots[SEQ // 2 + t * GROUP + n, 0:NBLK, :].astype(F32)
    small[...] = slots[:, NBLK:SLOT, :].astype(F32)
    pieces = [small[pl.ds(r * 8, 8), b, :][None] for r in range(8) for b in range(6)]
    plain = swap_groups(jnp.concatenate(pieces, axis=0))
    for r in range(8):
        ks[r // 4, pl.ds(r % 4, NBLK, stride=BLK), :] = plain[r * 6 : r * 6 + 6].reshape(NBLK, DH)
    for half in range(2):
        ks[half, QUART:SPAN, :] = pad
    for tile in range(2):
        first = tile * DH
        count = min(DH, QUART - first)
        there = slice(first, first + DH)
        k, v = ks[0, there, :], ks[1, there, :]
        allowed = causal(col_ref[there, :], row_ref[:, there], 0)
        out, dq, dk, dv = attend(
            qs[:, there, :].astype(BF16).reshape(QW, DH),
            gs[:, there, :].astype(BF16).reshape(QW, DH),
            k.astype(BF16),
            v.astype(BF16),
            k.T.astype(BF16),
            v.T.astype(BF16),
            jnp.concatenate([allowed] * GROUP, axis=1),
        )
        for n in range(GROUP):
            at = slice(n * DH, (n + 1) * DH)
            out_ref[first : first + count, at] = out[:, at].T[0:count].astype(BF16)
            dq_ref[first : first + count, at] = dq[:, at].T[0:count].astype(BF16)
        dk_ref[first : first + count, :] = dk[0:count].astype(BF16)
        dv_ref[first : first + count, :] = dv[0:count].astype(BF16)


def attend_tail(slots, seg_col, seg_row, partial):
    any_spec = pl.BlockSpec(memory_space=pl.ANY)
    last = lambda i: (3, 0)
    return pl.pallas_call(
        tail_kernel,
        grid=(1,),
        in_specs=[
            pl.BlockSpec((SEQ, SLOT, DH), lambda i: (0, 0, 0)),
            pl.BlockSpec((SPAN, 1), lambda i: (0, 0)),
            pl.BlockSpec((1, SPAN), lambda i: (0, 0)),
        ]
        + [any_spec] * 4,
        out_specs=[
            pl.BlockSpec((QUART, QW), last),
            pl.BlockSpec((QUART, QW), last),
            pl.BlockSpec((QUART, DH), last),
            pl.BlockSpec((QUART, DH), last),
        ],
        out_shape=OUT_SHAPES,
        input_output_aliases={3: 0, 4: 1, 5: 2, 6: 3},
        scratch_shapes=[
            pltpu.VMEM((GROUP, SPAN, DH), F32),
            pltpu.VMEM((GROUP, SPAN, DH), F32),
            pltpu.VMEM((2, SPAN, DH), F32),
            pltpu.VMEM((SEQ, 8, DH), F32),
        ],
        compiler_params=params(),
        cost_estimate=cost(6 * 2 * GROUP * QUART * DH * DH, 2_000_000, GROUP * QUART * DH),
        name="attend_tail",
    )(slots, seg_col, seg_row, *partial)


def after(values, *others):
    return lax.optimization_barrier((tuple(values), others))[0]


def on_device(queries, key_rows, value_rows, out_grad, mover_dest, segment_ids):
    me = lax.axis_index("head").astype(jnp.int32)
    held = (queries, key_rows, value_rows, out_grad)
    send = lambda x, *pairs: lax.ppermute(x, "head", list(pairs))
    exchange = lambda x: lax.all_to_all(x, "seq", split_axis=0, concat_axis=0, tiled=True)

    plan_row = mover_dest.reshape(1, NBLK)
    half = (SEQ // 2, SLOT, DH)
    one_lo, one_hi = pack(pack_one_kernel, "pack_one", 1, 1, [half] * 2, *held, plan_row)
    at_zero = send(one_lo, (3, 0))
    at_two = send(one_hi, (3, 2))
    rest = pack(pack_rest_kernel, "pack_rest", 4, 0, [(SEQ, SLOT, DH)] * 3, *held, plan_row)
    to_zero, to_two = send(rest[0], (3, 0)), send(rest[1], (3, 2))
    lo, hi = send(at_zero, (0, 1)), send(at_two, (2, 1))
    other = jnp.where(me == 3, rest[2], jnp.where(me == 0, to_zero, to_two))
    slots = jnp.where(me == 1, jnp.concatenate([lo, hi], axis=0), other)
    part = lambda shift: slice_group(*held, (me + shift) % 4)
    (slots, *slices) = after((slots, part(1), part(3), part(2)))

    pieces = exchange(slots)

    ahead, behind, across = after(slices, slots)
    two = send(across, (0, 2), (2, 0), (1, 3))
    plus = send(ahead, (0, 1), (1, 2), (2, 3))
    minus = send(behind, (1, 0), (2, 1), (0, 3))

    routed = route(pieces)
    stay = after((plus, minus, two), routed)
    seg_col = segment_ids.reshape(ROWS, 1)
    seg_row = segment_ids.reshape(1, ROWS)
    tail_seg = jnp.pad(segment_ids[STAY:], (0, SPAN - QUART), constant_values=-1)
    partial = attend_stay(me, held, stay, seg_col, seg_row)
    arrived = exchange(routed)
    return attend_tail(arrived, tail_seg.reshape(SPAN, 1), tail_seg.reshape(1, SPAN), partial)


def solution(mesh):
    rows = P(("seq", "head"), None)
    spread = P("seq", "head")
    return jax.shard_map(
        on_device,
        mesh=mesh,
        in_specs=(rows, rows, rows, rows, P("seq"), P("seq")),
        out_specs=(spread, spread, spread, spread),
        check_vma=False,
    )
```

```python
import math

import jax
import jax.numpy as jnp
from jax import lax
from jax.experimental import pallas as pl
from jax.experimental.pallas import tpu as pltpu
from jax.sharding import PartitionSpec as P

DH = 128
GROUP = 8
QW = GROUP * DH
ROWS = 768
QUART = 192
STAY = 576
BLK = 4
NBLK = 48
SEQ = 64
WIDE = 2 * QW + 2 * DH
SLOT = NBLK + 8
INV = 1.0 / math.sqrt(DH)
LOG2E = math.log2(math.e)
NEG = -1e30
F32 = jnp.float32
BF16 = jnp.bfloat16
VMEM_LIMIT = 56 * 1024 * 1024
SMALL_LIMIT = 24 * 1024 * 1024


def params(limit=VMEM_LIMIT):
    return pltpu.CompilerParams(vmem_limit_bytes=limit)


def cost(flops, bytes_accessed, transcendentals=0):
    return pl.CostEstimate(
        flops=flops, bytes_accessed=bytes_accessed, transcendentals=transcendentals
    )


def iota(shape, axis):
    return lax.broadcasted_iota(jnp.int32, shape, axis)


def swap_groups(x):
    sub = iota(x.shape, 1)
    grp = iota(x.shape, 2) // 16
    for bit in (1, 2, 4):
        s_on = (sub & bit) != 0
        l_on = (grp & bit) != 0
        up = pltpu.roll(pltpu.roll(x, 8 - bit, 1), 16 * bit, 2)
        down = pltpu.roll(pltpu.roll(x, bit, 1), 128 - 16 * bit, 2)
        x = jnp.where(s_on == l_on, x, jnp.where(l_on, up, down))
    return x


def pack_group(group, q_ref, k_ref, v_ref, g_ref, out, qs, ks, small):
    half = SEQ // 2
    thin = slice(group * DH, (group + 1) * DH)
    ks[0] = k_ref[:, thin].astype(F32)
    ks[1] = v_ref[:, thin].astype(F32)
    pieces = []
    for r in range(8):
        rows = ks[r // 4, pl.ds(r % 4, NBLK, stride=BLK), :]
        pieces.append(rows.reshape(6, 8, DH))
    mixed = swap_groups(jnp.concatenate(pieces, axis=0))
    for r in range(8):
        for b in range(6):
            small[pl.ds(r * 8, 8), b, :] = mixed[r * 6 + b]
    for which, src in enumerate((q_ref, g_ref)):
        dst = out[which]
        for n in range(GROUP):
            qs[n] = src[:, group * QW + n * DH : group * QW + (n + 1) * DH].astype(F32)
            for t in range(BLK):
                rows = qs[n, pl.ds(t, NBLK, stride=BLK), :]
                dst[t * GROUP + n, 0:NBLK, :] = rows.astype(BF16)
        dst[:, NBLK:SLOT, :] = small[pl.ds(which * half, half)].astype(BF16)


def put_plan(plan_ref, small):
    plan = jnp.concatenate([plan_ref[...], jnp.zeros((1, DH - NBLK), jnp.int32)], axis=1)
    small[:, 6, :] = jnp.broadcast_to((plan // 64).astype(F32), (SEQ, DH))
    small[:, 7, :] = jnp.broadcast_to((plan % 64).astype(F32), (SEQ, DH))


def pack_one_kernel(q_ref, k_ref, v_ref, g_ref, plan_ref, lo_ref, hi_ref, qs, ks, small):
    put_plan(plan_ref, small)
    pack_group(0, q_ref, k_ref, v_ref, g_ref, (lo_ref, hi_ref), qs, ks, small)


def pack_rest_kernel(q_ref, k_ref, v_ref, g_ref, plan_ref, o0, o2, o3, qs, ks, small):
    half = SEQ // 2
    put_plan(plan_ref, small)
    for group, out in ((0, o0), (2, o2), (3, o3)):
        halves = (out.at[0:half], out.at[half:SEQ])
        pack_group(group, q_ref, k_ref, v_ref, g_ref, halves, qs, ks, small)


def pack(kernel, name, width, first, shapes, queries, key_rows, value_rows, out_grad, plan_row):
    at = lambda i: (0, first)
    return pl.pallas_call(
        kernel,
        grid=(1,),
        in_specs=[
            pl.BlockSpec((QUART, width * QW), at),
            pl.BlockSpec((QUART, width * DH), at),
            pl.BlockSpec((QUART, width * DH), at),
            pl.BlockSpec((QUART, width * QW), at),
            pl.BlockSpec((1, NBLK), lambda i: (0, 0)),
        ],
        out_specs=[pl.BlockSpec(x, lambda i: (0, 0, 0)) for x in shapes],
        out_shape=[jax.ShapeDtypeStruct(x, BF16) for x in shapes],
        scratch_shapes=[
            pltpu.VMEM((GROUP, QUART, DH), F32),
            pltpu.VMEM((2, QUART, DH), F32),
            pltpu.VMEM((SEQ, 8, DH), F32),
        ],
        compiler_params=params(),
        cost_estimate=cost(0, 2_000_000 * len(shapes)),
        name=name,
    )(queries, key_rows, value_rows, out_grad, plan_row)


def slice_kernel(me_ref, q_ref, k_ref, v_ref, g_ref, o_ref):
    o_ref[:, 0:QW] = q_ref[...]
    o_ref[:, QW : 2 * QW] = g_ref[...]
    o_ref[:, 2 * QW : 2 * QW + DH] = k_ref[...]
    o_ref[:, 2 * QW + DH : WIDE] = v_ref[...]


def slice_group(queries, key_rows, value_rows, out_grad, group):
    column = lambda i, g: (0, g[0])
    return pl.pallas_call(
        slice_kernel,
        grid_spec=pltpu.PrefetchScalarGridSpec(
            num_scalar_prefetch=1,
            grid=(1,),
            in_specs=[
                pl.BlockSpec((QUART, QW), column),
                pl.BlockSpec((QUART, DH), column),
                pl.BlockSpec((QUART, DH), column),
                pl.BlockSpec((QUART, QW), column),
            ],
            out_specs=pl.BlockSpec((QUART, WIDE), lambda i, g: (0, 0)),
        ),
        out_shape=jax.ShapeDtypeStruct((QUART, WIDE), BF16),
        compiler_params=params(),
        cost_estimate=cost(0, 1_800_000),
        name="slice_group",
    )(group.reshape(1), queries, key_rows, value_rows, out_grad)


def plan_lines(tail):
    total = SEQ * NBLK
    col = iota((1, total), 1).astype(F32)
    owner = jnp.floor((col + 0.5) * (1.0 / NBLK))
    place = col - owner * NBLK
    pick = (iota((DH, total), 0).astype(F32) == place).astype(BF16)
    mine = iota((SEQ, total), 0).astype(F32) == owner
    lines = []
    for row in (6, 7):
        spread = jnp.dot(tail[:, row, :].astype(BF16), pick, preferred_element_type=F32)
        lines.append(jnp.sum(jnp.where(mine, spread, 0.0), axis=0, keepdims=True))
    return lines


def low_choice(line):
    return (iota((64, line.shape[1]), 0).astype(F32) == line).astype(BF16)


def choose(sel, low, line, first, runs):
    for k in range(runs):
        row = jnp.where(line == float(first + k), 1.0, 0.0).astype(BF16)
        sel[k * 64 : (k + 1) * 64, :] = low * row


PARTS = 4
TILE = SEQ * NBLK // PARTS
RUNS = TILE // 64
SHARDS = TILE // NBLK


def route_kernel(in_ref, out_ref, xs, ks, sel, low):
    tail = in_ref[:, NBLK:SLOT, :].astype(F32)
    high, digits = plan_lines(tail)
    low[...] = low_choice(digits)
    here = iota((NBLK, DH), 1) // 16 == iota((NBLK, DH), 0) % 8
    fold = (iota((DH, DH), 0) % 16 == iota((DH, DH), 1) % 16).astype(BF16)
    xs[:, 0:DH] = in_ref[:, 0:NBLK, :].reshape(SEQ * NBLK, DH)
    for s in range(SEQ):
        rows = [jnp.broadcast_to(tail[s, b : b + 1, :], (8, DH)) for b in range(6)]
        wide = jnp.where(here, jnp.concatenate(rows, axis=0), 0.0).astype(BF16)
        ks[s * NBLK : (s + 1) * NBLK, :] = wide
    xs[:, DH : 2 * DH] = jnp.dot(ks[...], fold, preferred_element_type=F32).astype(BF16)
    for p in range(PARTS):
        choose(sel.at[p % 2], low[...], high, p * RUNS, RUNS)
        got = jnp.dot(sel[p % 2], xs[...], preferred_element_type=F32)
        for d in range(SHARDS):
            part = got[d * NBLK : (d + 1) * NBLK]
            kept = jnp.where(here, part[:, DH : 2 * DH], 0.0)
            sums = [jnp.sum(kept[b * 8 : b * 8 + 8], axis=0, keepdims=True) for b in range(6)]
            sums.append(jnp.zeros((2, DH), F32))
            out_ref[p * SHARDS + d, 0:NBLK, :] = part[:, 0:DH].astype(BF16)
            out_ref[p * SHARDS + d, NBLK:SLOT, :] = jnp.concatenate(sums, axis=0).astype(BF16)


def route(slots):
    vmem = pl.BlockSpec(memory_space=pltpu.VMEM)
    return pl.pallas_call(
        route_kernel,
        in_specs=[vmem],
        out_specs=vmem,
        out_shape=pltpu.HBM((SEQ, SLOT, DH), BF16),
        scratch_shapes=[
            pltpu.VMEM((SEQ * NBLK, 2 * DH), BF16),
            pltpu.VMEM((SEQ * NBLK, DH), BF16),
            pltpu.VMEM((2, TILE, SEQ * NBLK), BF16),
            pltpu.VMEM((64, SEQ * NBLK), BF16),
        ],
        compiler_params=params(SMALL_LIMIT),
        cost_estimate=cost(4 * SEQ * NBLK * SEQ * NBLK * DH, 2_000_000),
        name="route",
    )(slots)


def dot(a, b, dims):
    return lax.dot_general(a, b, (dims, ((), ())), preferred_element_type=F32)


NT = ((1,), (1,))
NN = ((1,), (0,))


def attend(q, g, k, v, k_cols, v_cols, allowed):
    scores = jnp.where(allowed, dot(k, q, NT) * (INV * LOG2E), NEG)
    weights = jnp.exp2(scores - jnp.max(scores, axis=0, keepdims=True))
    probs = weights * (1.0 / jnp.sum(weights, axis=0, keepdims=True))
    probs_low = probs.astype(BF16)
    grad_probs = dot(v, g, NT)
    centre = jnp.sum(probs * grad_probs, axis=0, keepdims=True)
    grad_scores = (probs * (grad_probs - centre) * INV).astype(BF16)
    out_cols = dot(v_cols, probs_low, NN)
    dq_cols = dot(k_cols, grad_scores, NN)
    return out_cols, dq_cols, dot(grad_scores, q, NN), dot(probs_low, g, NN)


def causal(seg_col, seg_row, first):
    j = iota((seg_col.shape[0], DH), 0)
    i = iota((seg_col.shape[0], DH), 1) + first
    return (seg_col == seg_row) & (j <= i)


PAD = 640
PAIR = 2


def stay_kernel(
    me_ref, q_any, k_any, v_any, g_any, plus, minus, two, col_ref, row_ref,
    out_ref, dq_ref, dk_ref, dv_ref, rows, kt, vt, dk, dv, sems,
):
    me = me_ref[0]

    def fetch(src, part):
        pltpu.make_async_copy(src, rows.at[pl.ds(part * QUART, QUART), :], sems.at[part]).start()

    wide = pl.ds(pl.multiple_of(me * QW, QW), QW)
    thin = pl.ds(pl.multiple_of(me * DH, DH), DH)

    def own(part):
        there = pl.ds(part * QUART, QUART)
        columns = (0, QW, 2 * QW, 2 * QW + DH, WIDE)
        for n, (src, at) in enumerate(((q_any, wide), (g_any, wide), (k_any, thin), (v_any, thin))):
            pltpu.make_async_copy(
                src.at[:, at], rows.at[there, columns[n] : columns[n + 1]], sems.at[part]
            ).start()

    @pl.when(me == 0)
    def _():
        own(0)
        fetch(minus, 1)
        fetch(two, 2)

    @pl.when(me == 1)
    def _():
        fetch(plus, 0)
        own(1)
        fetch(minus, 2)

    @pl.when(me == 2)
    def _():
        fetch(two, 0)
        fetch(plus, 1)
        own(2)

    @pl.when(me == 3)
    def _():
        fetch(minus, 0)
        fetch(two, 1)
        fetch(plus, 2)

    dk[...] = jnp.zeros_like(dk)
    dv[...] = jnp.zeros_like(dv)
    rows[STAY:PAD, :] = jnp.zeros((PAD - STAY, WIDE), BF16)
    for part in range(3):
        pltpu.make_async_copy(plus, rows.at[pl.ds(part * QUART, QUART), :], sems.at[part]).wait()
    kt[...] = rows[:, 2 * QW : 2 * QW + DH].astype(F32).T.astype(BF16)
    vt[...] = rows[:, 2 * QW + DH : WIDE].astype(F32).T.astype(BF16)

    for tile in range(PAD // DH):
        width = (tile + 1) * DH
        there = slice(tile * DH, width)
        count = min(DH, STAY - tile * DH)
        allowed = causal(col_ref[0:width, :], row_ref[:, there], tile * DH)
        allowed = jnp.concatenate([allowed] * PAIR, axis=1)

        for first in range(0, GROUP, PAIR):
            heads = range(first, first + PAIR)
            q = [rows[there, n * DH : (n + 1) * DH] for n in heads]
            g = [rows[there, QW + n * DH : QW + (n + 1) * DH] for n in heads]
            out, dq, dk_part, dv_part = attend(
                jnp.concatenate(q, axis=0),
                jnp.concatenate(g, axis=0),
                rows[0:width, 2 * QW : 2 * QW + DH],
                rows[0:width, 2 * QW + DH : WIDE],
                kt[:, 0:width],
                vt[:, 0:width],
                allowed,
            )
            for h, n in enumerate(heads):
                at = slice(n * DH, (n + 1) * DH)
                columns = slice(h * DH, (h + 1) * DH)
                out_ref[tile * DH : tile * DH + count, at] = out[:, columns].T[0:count].astype(BF16)
                dq_ref[tile * DH : tile * DH + count, at] = dq[:, columns].T[0:count].astype(BF16)
            dk[0:width, :] += dk_part
            dv[0:width, :] += dv_part

    dk_ref[...] = dk[0:STAY, :].astype(BF16)
    dv_ref[...] = dv[0:STAY, :].astype(BF16)


OUT_SHAPES = [
    jax.ShapeDtypeStruct((ROWS, QW), BF16),
    jax.ShapeDtypeStruct((ROWS, QW), BF16),
    jax.ShapeDtypeStruct((ROWS, DH), BF16),
    jax.ShapeDtypeStruct((ROWS, DH), BF16),
]


def attend_stay(me, held, received, seg_col, seg_row):
    any_spec = pl.BlockSpec(memory_space=pl.ANY)
    top = lambda n, m: (0, 0)
    return pl.pallas_call(
        stay_kernel,
        grid_spec=pltpu.PrefetchScalarGridSpec(
            num_scalar_prefetch=1,
            grid=(1,),
            in_specs=[any_spec] * 7 + [pl.BlockSpec((ROWS, 1), top), pl.BlockSpec((1, ROWS), top)],
            out_specs=[
                pl.BlockSpec((STAY, QW), top),
                pl.BlockSpec((STAY, QW), top),
                pl.BlockSpec((STAY, DH), top),
                pl.BlockSpec((STAY, DH), top),
            ],
            scratch_shapes=[
                pltpu.VMEM((PAD, WIDE), BF16),
                pltpu.VMEM((DH, PAD), BF16),
                pltpu.VMEM((DH, PAD), BF16),
                pltpu.VMEM((PAD, DH), F32),
                pltpu.VMEM((PAD, DH), F32),
                pltpu.SemaphoreType.DMA((3,)),
            ],
        ),
        out_shape=OUT_SHAPES,
        compiler_params=params(),
        cost_estimate=cost(60 * 2 * GROUP * STAY * STAY * DH, 6_000_000, GROUP * STAY * STAY),
        name="attend_stay",
    )(me.reshape(1), *held, *received, seg_col, seg_row)


SPAN = 2 * DH


def tail_kernel(
    slots, col_ref, row_ref, a0, a1, a2, a3, out_ref, dq_ref, dk_ref, dv_ref, qs, gs, ks, small
):
    pad = jnp.zeros((SPAN - QUART, DH), F32)
    for n in range(GROUP):
        qs[n, QUART:SPAN, :] = pad
        gs[n, QUART:SPAN, :] = pad
        for t in range(BLK):
            there = pl.ds(t, NBLK, stride=BLK)
            qs[n, there, :] = slots[t * GROUP + n, 0:NBLK, :].astype(F32)
            gs[n, there, :] = slots[SEQ // 2 + t * GROUP + n, 0:NBLK, :].astype(F32)
    small[...] = slots[:, NBLK:SLOT, :].astype(F32)
    pieces = [small[pl.ds(r * 8, 8), b, :][None] for r in range(8) for b in range(6)]
    plain = swap_groups(jnp.concatenate(pieces, axis=0))
    for r in range(8):
        ks[r // 4, pl.ds(r % 4, NBLK, stride=BLK), :] = plain[r * 6 : r * 6 + 6].reshape(NBLK, DH)
    for half in range(2):
        ks[half, QUART:SPAN, :] = pad
    for tile in range(2):
        first = tile * DH
        count = min(DH, QUART - first)
        there = slice(first, first + DH)
        k, v = ks[0, there, :], ks[1, there, :]
        allowed = causal(col_ref[there, :], row_ref[:, there], 0)
        out, dq, dk, dv = attend(
            qs[:, there, :].astype(BF16).reshape(QW, DH),
            gs[:, there, :].astype(BF16).reshape(QW, DH),
            k.astype(BF16),
            v.astype(BF16),
            k.T.astype(BF16),
            v.T.astype(BF16),
            jnp.concatenate([allowed] * GROUP, axis=1),
        )
        for n in range(GROUP):
            at = slice(n * DH, (n + 1) * DH)
            out_ref[first : first + count, at] = out[:, at].T[0:count].astype(BF16)
            dq_ref[first : first + count, at] = dq[:, at].T[0:count].astype(BF16)
        dk_ref[first : first + count, :] = dk[0:count].astype(BF16)
        dv_ref[first : first + count, :] = dv[0:count].astype(BF16)


def attend_tail(slots, seg_col, seg_row, partial):
    any_spec = pl.BlockSpec(memory_space=pl.ANY)
    last = lambda i: (3, 0)
    return pl.pallas_call(
        tail_kernel,
        grid=(1,),
        in_specs=[
            pl.BlockSpec((SEQ, SLOT, DH), lambda i: (0, 0, 0)),
            pl.BlockSpec((SPAN, 1), lambda i: (0, 0)),
            pl.BlockSpec((1, SPAN), lambda i: (0, 0)),
        ]
        + [any_spec] * 4,
        out_specs=[
            pl.BlockSpec((QUART, QW), last),
            pl.BlockSpec((QUART, QW), last),
            pl.BlockSpec((QUART, DH), last),
            pl.BlockSpec((QUART, DH), last),
        ],
        out_shape=OUT_SHAPES,
        input_output_aliases={3: 0, 4: 1, 5: 2, 6: 3},
        scratch_shapes=[
            pltpu.VMEM((GROUP, SPAN, DH), F32),
            pltpu.VMEM((GROUP, SPAN, DH), F32),
            pltpu.VMEM((2, SPAN, DH), F32),
            pltpu.VMEM((SEQ, 8, DH), F32),
        ],
        compiler_params=params(SMALL_LIMIT),
        cost_estimate=cost(6 * 2 * GROUP * QUART * DH * DH, 2_000_000, GROUP * QUART * DH),
        name="attend_tail",
    )(slots, seg_col, seg_row, *partial)


def after(values, *others):
    return lax.optimization_barrier((tuple(values), others))[0]


def on_device(queries, key_rows, value_rows, out_grad, mover_dest, segment_ids):
    me = lax.axis_index("head").astype(jnp.int32)
    held = (queries, key_rows, value_rows, out_grad)
    send = lambda x, *pairs: lax.ppermute(x, "head", list(pairs))
    exchange = lambda x: lax.all_to_all(x, "seq", split_axis=0, concat_axis=0, tiled=True)

    plan_row = mover_dest.reshape(1, NBLK)
    half = (SEQ // 2, SLOT, DH)
    one_lo, one_hi = pack(pack_one_kernel, "pack_one", 1, 1, [half] * 2, *held, plan_row)
    at_zero = send(one_lo, (3, 0))
    at_two = send(one_hi, (3, 2))
    rest = pack(pack_rest_kernel, "pack_rest", 4, 0, [(SEQ, SLOT, DH)] * 3, *held, plan_row)
    to_zero, to_two = send(rest[0], (3, 0)), send(rest[1], (3, 2))
    lo, hi = send(at_zero, (0, 1)), send(at_two, (2, 1))
    other = jnp.where(me == 3, rest[2], jnp.where(me == 0, to_zero, to_two))
    slots = jnp.where(me == 1, jnp.concatenate([lo, hi], axis=0), other)
    part = lambda shift: slice_group(*held, (me + shift) % 4)
    (slots, *slices) = after((slots, part(1), part(3), part(2)))

    pieces = exchange(slots)

    ahead, behind, across = after(slices, slots)
    two = send(across, (0, 2), (2, 0), (1, 3))
    plus = send(ahead, (0, 1), (1, 2), (2, 3))
    minus = send(behind, (1, 0), (2, 1), (0, 3))

    routed = route(pieces)
    stay = after((plus, minus, two), routed)
    seg_col = segment_ids.reshape(ROWS, 1)
    seg_row = segment_ids.reshape(1, ROWS)
    tail_seg = jnp.pad(segment_ids[STAY:], (0, SPAN - QUART), constant_values=-1)
    partial = attend_stay(me, held, stay, seg_col, seg_row)
    arrived = exchange(routed)
    return attend_tail(arrived, tail_seg.reshape(SPAN, 1), tail_seg.reshape(1, SPAN), partial)


def solution(mesh):
    rows = P(("seq", "head"), None)
    spread = P("seq", "head")
    return jax.shard_map(
        on_device,
        mesh=mesh,
        in_specs=(rows, rows, rows, rows, P("seq"), P("seq")),
        out_specs=(spread, spread, spread, spread),
        check_vma=False,
    )
```

```python
import math

import jax
import jax.numpy as jnp
from jax import lax
from jax.experimental import pallas as pl
from jax.experimental.pallas import tpu as pltpu
from jax.sharding import PartitionSpec as P

DH = 128
GROUP = 8
QW = GROUP * DH
ROWS = 768
QUART = 192
STAY = 576
BLK = 4
NBLK = 48
SEQ = 64
WIDE = 2 * QW + 2 * DH
SLOT = NBLK + 8
INV = 1.0 / math.sqrt(DH)
LOG2E = math.log2(math.e)
NEG = -1e30
F32 = jnp.float32
BF16 = jnp.bfloat16
VMEM_LIMIT = 56 * 1024 * 1024
SMALL_LIMIT = 24 * 1024 * 1024


def params(limit=VMEM_LIMIT):
    return pltpu.CompilerParams(vmem_limit_bytes=limit)


def cost(flops, bytes_accessed, transcendentals=0):
    return pl.CostEstimate(
        flops=flops, bytes_accessed=bytes_accessed, transcendentals=transcendentals
    )


def iota(shape, axis):
    return lax.broadcasted_iota(jnp.int32, shape, axis)


def swap_groups(x):
    sub = iota(x.shape, 1)
    grp = iota(x.shape, 2) // 16
    for bit in (1, 2, 4):
        s_on = (sub & bit) != 0
        l_on = (grp & bit) != 0
        up = pltpu.roll(pltpu.roll(x, 8 - bit, 1), 16 * bit, 2)
        down = pltpu.roll(pltpu.roll(x, bit, 1), 128 - 16 * bit, 2)
        x = jnp.where(s_on == l_on, x, jnp.where(l_on, up, down))
    return x


def pack_group(group, q_ref, k_ref, v_ref, g_ref, out, qs, ks, small):
    half = SEQ // 2
    thin = slice(group * DH, (group + 1) * DH)
    ks[0] = k_ref[:, thin].astype(F32)
    ks[1] = v_ref[:, thin].astype(F32)
    pieces = []
    for r in range(8):
        rows = ks[r // 4, pl.ds(r % 4, NBLK, stride=BLK), :]
        pieces.append(rows.reshape(6, 8, DH))
    mixed = swap_groups(jnp.concatenate(pieces, axis=0))
    for r in range(8):
        for b in range(6):
            small[pl.ds(r * 8, 8), b, :] = mixed[r * 6 + b]
    for which, src in enumerate((q_ref, g_ref)):
        dst = out[which]
        for n in range(GROUP):
            qs[n] = src[:, group * QW + n * DH : group * QW + (n + 1) * DH].astype(F32)
            for t in range(BLK):
                rows = qs[n, pl.ds(t, NBLK, stride=BLK), :]
                dst[t * GROUP + n, 0:NBLK, :] = rows.astype(BF16)
        dst[:, NBLK:SLOT, :] = small[pl.ds(which * half, half)].astype(BF16)


def put_plan(plan_ref, small):
    plan = jnp.concatenate([plan_ref[...], jnp.zeros((1, DH - NBLK), jnp.int32)], axis=1)
    small[:, 6, :] = jnp.broadcast_to((plan // 64).astype(F32), (SEQ, DH))
    small[:, 7, :] = jnp.broadcast_to((plan % 64).astype(F32), (SEQ, DH))


def pack_one_kernel(q_ref, k_ref, v_ref, g_ref, plan_ref, lo_ref, hi_ref, qs, ks, small):
    put_plan(plan_ref, small)
    pack_group(0, q_ref, k_ref, v_ref, g_ref, (lo_ref, hi_ref), qs, ks, small)


def pack_rest_kernel(q_ref, k_ref, v_ref, g_ref, plan_ref, o0, o2, o3, qs, ks, small):
    half = SEQ // 2
    put_plan(plan_ref, small)
    for group, out in ((0, o0), (2, o2), (3, o3)):
        halves = (out.at[0:half], out.at[half:SEQ])
        pack_group(group, q_ref, k_ref, v_ref, g_ref, halves, qs, ks, small)


def pack(kernel, name, width, first, shapes, queries, key_rows, value_rows, out_grad, plan_row):
    at = lambda i: (0, first)
    return pl.pallas_call(
        kernel,
        grid=(1,),
        in_specs=[
            pl.BlockSpec((QUART, width * QW), at),
            pl.BlockSpec((QUART, width * DH), at),
            pl.BlockSpec((QUART, width * DH), at),
            pl.BlockSpec((QUART, width * QW), at),
            pl.BlockSpec((1, NBLK), lambda i: (0, 0)),
        ],
        out_specs=[pl.BlockSpec(x, lambda i: (0, 0, 0)) for x in shapes],
        out_shape=[jax.ShapeDtypeStruct(x, BF16) for x in shapes],
        scratch_shapes=[
            pltpu.VMEM((GROUP, QUART, DH), F32),
            pltpu.VMEM((2, QUART, DH), F32),
            pltpu.VMEM((SEQ, 8, DH), F32),
        ],
        compiler_params=params(),
        cost_estimate=cost(0, 2_000_000 * len(shapes)),
        name=name,
    )(queries, key_rows, value_rows, out_grad, plan_row)


def slice_kernel(me_ref, q_ref, k_ref, v_ref, g_ref, o_ref):
    o_ref[:, 0:QW] = q_ref[...]
    o_ref[:, QW : 2 * QW] = g_ref[...]
    o_ref[:, 2 * QW : 2 * QW + DH] = k_ref[...]
    o_ref[:, 2 * QW + DH : WIDE] = v_ref[...]


def slice_group(queries, key_rows, value_rows, out_grad, group):
    column = lambda i, g: (0, g[0])
    return pl.pallas_call(
        slice_kernel,
        grid_spec=pltpu.PrefetchScalarGridSpec(
            num_scalar_prefetch=1,
            grid=(1,),
            in_specs=[
                pl.BlockSpec((QUART, QW), column),
                pl.BlockSpec((QUART, DH), column),
                pl.BlockSpec((QUART, DH), column),
                pl.BlockSpec((QUART, QW), column),
            ],
            out_specs=pl.BlockSpec((QUART, WIDE), lambda i, g: (0, 0)),
        ),
        out_shape=jax.ShapeDtypeStruct((QUART, WIDE), BF16),
        compiler_params=params(),
        cost_estimate=cost(0, 1_800_000),
        name="slice_group",
    )(group.reshape(1), queries, key_rows, value_rows, out_grad)


def plan_lines(tail):
    total = SEQ * NBLK
    col = iota((1, total), 1).astype(F32)
    owner = jnp.floor((col + 0.5) * (1.0 / NBLK))
    place = col - owner * NBLK
    pick = (iota((DH, total), 0).astype(F32) == place).astype(BF16)
    mine = iota((SEQ, total), 0).astype(F32) == owner
    lines = []
    for row in (6, 7):
        spread = jnp.dot(tail[:, row, :].astype(BF16), pick, preferred_element_type=F32)
        lines.append(jnp.sum(jnp.where(mine, spread, 0.0), axis=0, keepdims=True))
    return lines


def low_choice(line):
    return (iota((64, line.shape[1]), 0).astype(F32) == line).astype(BF16)


def choose(sel, low, line, first, runs):
    for k in range(runs):
        row = jnp.where(line == float(first + k), 1.0, 0.0).astype(BF16)
        sel[k * 64 : (k + 1) * 64, :] = low * row


PARTS = 4
TILE = SEQ * NBLK // PARTS
RUNS = TILE // 64
SHARDS = TILE // NBLK


def route_kernel(in_ref, out_ref, xs, ks, sel, low):
    tail = in_ref[:, NBLK:SLOT, :].astype(F32)
    high, digits = plan_lines(tail)
    low[...] = low_choice(digits)
    here = iota((NBLK, DH), 1) // 16 == iota((NBLK, DH), 0) % 8
    fold = (iota((DH, DH), 0) % 16 == iota((DH, DH), 1) % 16).astype(BF16)
    xs[:, 0:DH] = in_ref[:, 0:NBLK, :].reshape(SEQ * NBLK, DH)
    for s in range(SEQ):
        rows = [jnp.broadcast_to(tail[s, b : b + 1, :], (8, DH)) for b in range(6)]
        wide = jnp.where(here, jnp.concatenate(rows, axis=0), 0.0).astype(BF16)
        ks[s * NBLK : (s + 1) * NBLK, :] = wide
    xs[:, DH : 2 * DH] = jnp.dot(ks[...], fold, preferred_element_type=F32).astype(BF16)
    for p in range(PARTS):
        choose(sel.at[p % 2], low[...], high, p * RUNS, RUNS)
        got = jnp.dot(sel[p % 2], xs[...], preferred_element_type=F32)
        for d in range(SHARDS):
            part = got[d * NBLK : (d + 1) * NBLK]
            kept = jnp.where(here, part[:, DH : 2 * DH], 0.0)
            sums = [jnp.sum(kept[b * 8 : b * 8 + 8], axis=0, keepdims=True) for b in range(6)]
            sums.append(jnp.zeros((2, DH), F32))
            out_ref[p * SHARDS + d, 0:NBLK, :] = part[:, 0:DH].astype(BF16)
            out_ref[p * SHARDS + d, NBLK:SLOT, :] = jnp.concatenate(sums, axis=0).astype(BF16)


def route(slots):
    vmem = pl.BlockSpec(memory_space=pltpu.VMEM)
    return pl.pallas_call(
        route_kernel,
        in_specs=[vmem],
        out_specs=vmem,
        out_shape=pltpu.HBM((SEQ, SLOT, DH), BF16),
        scratch_shapes=[
            pltpu.VMEM((SEQ * NBLK, 2 * DH), BF16),
            pltpu.VMEM((SEQ * NBLK, DH), BF16),
            pltpu.VMEM((2, TILE, SEQ * NBLK), BF16),
            pltpu.VMEM((64, SEQ * NBLK), BF16),
        ],
        compiler_params=params(SMALL_LIMIT),
        cost_estimate=cost(4 * SEQ * NBLK * SEQ * NBLK * DH, 2_000_000),
        name="route",
    )(slots)


def dot(a, b, dims):
    return lax.dot_general(a, b, (dims, ((), ())), preferred_element_type=F32)


NT = ((1,), (1,))
NN = ((1,), (0,))


def attend(q, g, k, v, k_cols, v_cols, allowed):
    scores = jnp.where(allowed, dot(k, q, NT) * (INV * LOG2E), NEG)
    weights = jnp.exp2(scores - jnp.max(scores, axis=0, keepdims=True))
    probs = weights * (1.0 / jnp.sum(weights, axis=0, keepdims=True))
    probs_low = probs.astype(BF16)
    grad_probs = dot(v, g, NT)
    centre = jnp.sum(probs * grad_probs, axis=0, keepdims=True)
    grad_scores = (probs * (grad_probs - centre) * INV).astype(BF16)
    out_cols = dot(v_cols, probs_low, NN)
    dq_cols = dot(k_cols, grad_scores, NN)
    return out_cols, dq_cols, dot(grad_scores, q, NN), dot(probs_low, g, NN)


def causal(seg_col, seg_row, first):
    j = iota((seg_col.shape[0], DH), 0)
    i = iota((seg_col.shape[0], DH), 1) + first
    return (seg_col == seg_row) & (j <= i)


PAD = 640
PAIR = 8


def stay_kernel(
    me_ref, q_any, k_any, v_any, g_any, plus, minus, two, col_ref, row_ref,
    out_ref, dq_ref, dk_ref, dv_ref, rows, kt, vt, dk, dv, sems,
):
    me = me_ref[0]

    def fetch(src, part):
        pltpu.make_async_copy(src, rows.at[pl.ds(part * QUART, QUART), :], sems.at[part]).start()

    wide = pl.ds(pl.multiple_of(me * QW, QW), QW)
    thin = pl.ds(pl.multiple_of(me * DH, DH), DH)

    def own(part):
        there = pl.ds(part * QUART, QUART)
        columns = (0, QW, 2 * QW, 2 * QW + DH, WIDE)
        for n, (src, at) in enumerate(((q_any, wide), (g_any, wide), (k_any, thin), (v_any, thin))):
            pltpu.make_async_copy(
                src.at[:, at], rows.at[there, columns[n] : columns[n + 1]], sems.at[part]
            ).start()

    @pl.when(me == 0)
    def _():
        own(0)
        fetch(minus, 1)
        fetch(two, 2)

    @pl.when(me == 1)
    def _():
        fetch(plus, 0)
        own(1)
        fetch(minus, 2)

    @pl.when(me == 2)
    def _():
        fetch(two, 0)
        fetch(plus, 1)
        own(2)

    @pl.when(me == 3)
    def _():
        fetch(minus, 0)
        fetch(two, 1)
        fetch(plus, 2)

    dk[...] = jnp.zeros_like(dk)
    dv[...] = jnp.zeros_like(dv)
    rows[STAY:PAD, :] = jnp.zeros((PAD - STAY, WIDE), BF16)
    for part in range(3):
        pltpu.make_async_copy(plus, rows.at[pl.ds(part * QUART, QUART), :], sems.at[part]).wait()
    kt[...] = rows[:, 2 * QW : 2 * QW + DH].astype(F32).T.astype(BF16)
    vt[...] = rows[:, 2 * QW + DH : WIDE].astype(F32).T.astype(BF16)

    for tile in range(PAD // DH):
        width = (tile + 1) * DH
        there = slice(tile * DH, width)
        count = min(DH, STAY - tile * DH)
        allowed = causal(col_ref[0:width, :], row_ref[:, there], tile * DH)
        allowed = jnp.concatenate([allowed] * PAIR, axis=1)

        for first in range(0, GROUP, PAIR):
            heads = range(first, first + PAIR)
            q = [rows[there, n * DH : (n + 1) * DH] for n in heads]
            g = [rows[there, QW + n * DH : QW + (n + 1) * DH] for n in heads]
            out, dq, dk_part, dv_part = attend(
                jnp.concatenate(q, axis=0),
                jnp.concatenate(g, axis=0),
                rows[0:width, 2 * QW : 2 * QW + DH],
                rows[0:width, 2 * QW + DH : WIDE],
                kt[:, 0:width],
                vt[:, 0:width],
                allowed,
            )
            for h, n in enumerate(heads):
                at = slice(n * DH, (n + 1) * DH)
                columns = slice(h * DH, (h + 1) * DH)
                out_ref[tile * DH : tile * DH + count, at] = out[:, columns].T[0:count].astype(BF16)
                dq_ref[tile * DH : tile * DH + count, at] = dq[:, columns].T[0:count].astype(BF16)
            dk[0:width, :] += dk_part
            dv[0:width, :] += dv_part

    dk_ref[...] = dk[0:STAY, :].astype(BF16)
    dv_ref[...] = dv[0:STAY, :].astype(BF16)


OUT_SHAPES = [
    jax.ShapeDtypeStruct((ROWS, QW), BF16),
    jax.ShapeDtypeStruct((ROWS, QW), BF16),
    jax.ShapeDtypeStruct((ROWS, DH), BF16),
    jax.ShapeDtypeStruct((ROWS, DH), BF16),
]


def attend_stay(me, held, received, seg_col, seg_row):
    any_spec = pl.BlockSpec(memory_space=pl.ANY)
    top = lambda n, m: (0, 0)
    return pl.pallas_call(
        stay_kernel,
        grid_spec=pltpu.PrefetchScalarGridSpec(
            num_scalar_prefetch=1,
            grid=(1,),
            in_specs=[any_spec] * 7 + [pl.BlockSpec((ROWS, 1), top), pl.BlockSpec((1, ROWS), top)],
            out_specs=[
                pl.BlockSpec((STAY, QW), top),
                pl.BlockSpec((STAY, QW), top),
                pl.BlockSpec((STAY, DH), top),
                pl.BlockSpec((STAY, DH), top),
            ],
            scratch_shapes=[
                pltpu.VMEM((PAD, WIDE), BF16),
                pltpu.VMEM((DH, PAD), BF16),
                pltpu.VMEM((DH, PAD), BF16),
                pltpu.VMEM((PAD, DH), F32),
                pltpu.VMEM((PAD, DH), F32),
                pltpu.SemaphoreType.DMA((3,)),
            ],
        ),
        out_shape=OUT_SHAPES,
        compiler_params=params(),
        cost_estimate=cost(60 * 2 * GROUP * STAY * STAY * DH, 6_000_000, GROUP * STAY * STAY),
        name="attend_stay",
    )(me.reshape(1), *held, *received, seg_col, seg_row)


SPAN = 2 * DH


def tail_kernel(
    slots, col_ref, row_ref, a0, a1, a2, a3, out_ref, dq_ref, dk_ref, dv_ref, qs, gs, ks, small
):
    pad = jnp.zeros((SPAN - QUART, DH), F32)
    for n in range(GROUP):
        qs[n, QUART:SPAN, :] = pad
        gs[n, QUART:SPAN, :] = pad
        for t in range(BLK):
            there = pl.ds(t, NBLK, stride=BLK)
            qs[n, there, :] = slots[t * GROUP + n, 0:NBLK, :].astype(F32)
            gs[n, there, :] = slots[SEQ // 2 + t * GROUP + n, 0:NBLK, :].astype(F32)
    small[...] = slots[:, NBLK:SLOT, :].astype(F32)
    pieces = [small[pl.ds(r * 8, 8), b, :][None] for r in range(8) for b in range(6)]
    plain = swap_groups(jnp.concatenate(pieces, axis=0))
    for r in range(8):
        ks[r // 4, pl.ds(r % 4, NBLK, stride=BLK), :] = plain[r * 6 : r * 6 + 6].reshape(NBLK, DH)
    for half in range(2):
        ks[half, QUART:SPAN, :] = pad
    for tile in range(2):
        first = tile * DH
        count = min(DH, QUART - first)
        there = slice(first, first + DH)
        k, v = ks[0, there, :], ks[1, there, :]
        allowed = causal(col_ref[there, :], row_ref[:, there], 0)
        out, dq, dk, dv = attend(
            qs[:, there, :].astype(BF16).reshape(QW, DH),
            gs[:, there, :].astype(BF16).reshape(QW, DH),
            k.astype(BF16),
            v.astype(BF16),
            k.T.astype(BF16),
            v.T.astype(BF16),
            jnp.concatenate([allowed] * GROUP, axis=1),
        )
        for n in range(GROUP):
            at = slice(n * DH, (n + 1) * DH)
            out_ref[first : first + count, at] = out[:, at].T[0:count].astype(BF16)
            dq_ref[first : first + count, at] = dq[:, at].T[0:count].astype(BF16)
        dk_ref[first : first + count, :] = dk[0:count].astype(BF16)
        dv_ref[first : first + count, :] = dv[0:count].astype(BF16)


def attend_tail(slots, seg_col, seg_row, partial):
    any_spec = pl.BlockSpec(memory_space=pl.ANY)
    last = lambda i: (3, 0)
    return pl.pallas_call(
        tail_kernel,
        grid=(1,),
        in_specs=[
            pl.BlockSpec((SEQ, SLOT, DH), lambda i: (0, 0, 0)),
            pl.BlockSpec((SPAN, 1), lambda i: (0, 0)),
            pl.BlockSpec((1, SPAN), lambda i: (0, 0)),
        ]
        + [any_spec] * 4,
        out_specs=[
            pl.BlockSpec((QUART, QW), last),
            pl.BlockSpec((QUART, QW), last),
            pl.BlockSpec((QUART, DH), last),
            pl.BlockSpec((QUART, DH), last),
        ],
        out_shape=OUT_SHAPES,
        input_output_aliases={3: 0, 4: 1, 5: 2, 6: 3},
        scratch_shapes=[
            pltpu.VMEM((GROUP, SPAN, DH), F32),
            pltpu.VMEM((GROUP, SPAN, DH), F32),
            pltpu.VMEM((2, SPAN, DH), F32),
            pltpu.VMEM((SEQ, 8, DH), F32),
        ],
        compiler_params=params(SMALL_LIMIT),
        cost_estimate=cost(6 * 2 * GROUP * QUART * DH * DH, 2_000_000, GROUP * QUART * DH),
        name="attend_tail",
    )(slots, seg_col, seg_row, *partial)


def after(values, *others):
    return lax.optimization_barrier((tuple(values), others))[0]


def on_device(queries, key_rows, value_rows, out_grad, mover_dest, segment_ids):
    me = lax.axis_index("head").astype(jnp.int32)
    held = (queries, key_rows, value_rows, out_grad)
    send = lambda x, *pairs: lax.ppermute(x, "head", list(pairs))
    exchange = lambda x: lax.all_to_all(x, "seq", split_axis=0, concat_axis=0, tiled=True)

    plan_row = mover_dest.reshape(1, NBLK)
    half = (SEQ // 2, SLOT, DH)
    one_lo, one_hi = pack(pack_one_kernel, "pack_one", 1, 1, [half] * 2, *held, plan_row)
    at_zero = send(one_lo, (3, 0))
    at_two = send(one_hi, (3, 2))
    rest = pack(pack_rest_kernel, "pack_rest", 4, 0, [(SEQ, SLOT, DH)] * 3, *held, plan_row)
    to_zero, to_two = send(rest[0], (3, 0)), send(rest[1], (3, 2))
    lo, hi = send(at_zero, (0, 1)), send(at_two, (2, 1))
    other = jnp.where(me == 3, rest[2], jnp.where(me == 0, to_zero, to_two))
    slots = jnp.where(me == 1, jnp.concatenate([lo, hi], axis=0), other)
    part = lambda shift: slice_group(*held, (me + shift) % 4)
    (slots, *slices) = after((slots, part(1), part(3), part(2)))

    pieces = exchange(slots)

    ahead, behind, across = after(slices, slots)
    two = send(across, (0, 2), (2, 0), (1, 3))
    plus = send(ahead, (0, 1), (1, 2), (2, 3))
    minus = send(behind, (1, 0), (2, 1), (0, 3))

    routed = route(pieces)
    stay = after((plus, minus, two), routed)
    seg_col = segment_ids.reshape(ROWS, 1)
    seg_row = segment_ids.reshape(1, ROWS)
    tail_seg = jnp.pad(segment_ids[STAY:], (0, SPAN - QUART), constant_values=-1)
    partial = attend_stay(me, held, stay, seg_col, seg_row)
    arrived = exchange(routed)
    return attend_tail(arrived, tail_seg.reshape(SPAN, 1), tail_seg.reshape(1, SPAN), partial)


def solution(mesh):
    rows = P(("seq", "head"), None)
    spread = P("seq", "head")
    return jax.shard_map(
        on_device,
        mesh=mesh,
        in_specs=(rows, rows, rows, rows, P("seq"), P("seq")),
        out_specs=(spread, spread, spread, spread),
        check_vma=False,
    )
```

```python
import math

import jax
import jax.numpy as jnp
from jax import lax
from jax.experimental import pallas as pl
from jax.experimental.pallas import tpu as pltpu
from jax.sharding import PartitionSpec as P

DH = 128
GROUP = 8
QW = GROUP * DH
ROWS = 768
QUART = 192
STAY = 576
BLK = 4
NBLK = 48
SEQ = 64
WIDE = 2 * QW + 2 * DH
SLOT = NBLK + 8
INV = 1.0 / math.sqrt(DH)
LOG2E = math.log2(math.e)
NEG = -1e30
F32 = jnp.float32
BF16 = jnp.bfloat16
VMEM_LIMIT = 56 * 1024 * 1024
SMALL_LIMIT = 24 * 1024 * 1024


def params(limit=VMEM_LIMIT):
    return pltpu.CompilerParams(vmem_limit_bytes=limit)


def cost(flops, bytes_accessed, transcendentals=0):
    return pl.CostEstimate(
        flops=flops, bytes_accessed=bytes_accessed, transcendentals=transcendentals
    )


def iota(shape, axis):
    return lax.broadcasted_iota(jnp.int32, shape, axis)


def swap_groups(x):
    sub = iota(x.shape, 1)
    grp = iota(x.shape, 2) // 16
    for bit in (1, 2, 4):
        s_on = (sub & bit) != 0
        l_on = (grp & bit) != 0
        up = pltpu.roll(pltpu.roll(x, 8 - bit, 1), 16 * bit, 2)
        down = pltpu.roll(pltpu.roll(x, bit, 1), 128 - 16 * bit, 2)
        x = jnp.where(s_on == l_on, x, jnp.where(l_on, up, down))
    return x


def pack_group(group, q_ref, k_ref, v_ref, g_ref, out, qs, ks, small):
    half = SEQ // 2
    thin = slice(group * DH, (group + 1) * DH)
    ks[0, 0:QUART, :] = k_ref[:, thin].astype(F32)
    ks[1, 0:QUART, :] = v_ref[:, thin].astype(F32)
    pieces = []
    for r in range(8):
        rows = ks[r // 4, pl.ds(r % 4, NBLK, stride=BLK), :]
        pieces.append(rows.reshape(6, 8, DH))
    mixed = swap_groups(jnp.concatenate(pieces, axis=0))
    for r in range(8):
        for b in range(6):
            small[pl.ds(r * 8, 8), b, :] = mixed[r * 6 + b]
    for which, src in enumerate((q_ref, g_ref)):
        dst = out[which]
        for n in range(GROUP):
            qs[n, 0:QUART, :] = src[:, group * QW + n * DH : group * QW + (n + 1) * DH].astype(F32)
            for t in range(BLK):
                rows = qs[n, pl.ds(t, NBLK, stride=BLK), :]
                dst[t * GROUP + n, 0:NBLK, :] = rows.astype(BF16)
        dst[:, NBLK:SLOT, :] = small[pl.ds(which * half, half)].astype(BF16)


def put_plan(plan_ref, small):
    plan = jnp.concatenate([plan_ref[...], jnp.zeros((1, DH - NBLK), jnp.int32)], axis=1)
    small[:, 6, :] = jnp.broadcast_to((plan // 64).astype(F32), (SEQ, DH))
    small[:, 7, :] = jnp.broadcast_to((plan % 64).astype(F32), (SEQ, DH))


def pack_one_kernel(q_ref, k_ref, v_ref, g_ref, plan_ref, lo_ref, hi_ref, qs, ks, small):
    put_plan(plan_ref, small)
    pack_group(0, q_ref, k_ref, v_ref, g_ref, (lo_ref, hi_ref), qs, ks, small)


def pack_rest_kernel(q_ref, k_ref, v_ref, g_ref, plan_ref, o0, o2, o3, qs, ks, small):
    half = SEQ // 2
    put_plan(plan_ref, small)
    for group, out in ((0, o0), (2, o2), (3, o3)):
        halves = (out.at[0:half], out.at[half:SEQ])
        pack_group(group, q_ref, k_ref, v_ref, g_ref, halves, qs, ks, small)


def pack(kernel, name, width, first, shapes, queries, key_rows, value_rows, out_grad, plan_row):
    at = lambda i: (0, first)
    return pl.pallas_call(
        kernel,
        grid=(1,),
        in_specs=[
            pl.BlockSpec((QUART, width * QW), at),
            pl.BlockSpec((QUART, width * DH), at),
            pl.BlockSpec((QUART, width * DH), at),
            pl.BlockSpec((QUART, width * QW), at),
            pl.BlockSpec((1, NBLK), lambda i: (0, 0)),
        ],
        out_specs=[pl.BlockSpec(x, lambda i: (0, 0, 0)) for x in shapes],
        out_shape=[jax.ShapeDtypeStruct(x, BF16) for x in shapes],
        scratch_shapes=[
            pltpu.VMEM((GROUP, QUART + 8, DH), F32),
            pltpu.VMEM((2, QUART + 8, DH), F32),
            pltpu.VMEM((SEQ, 8, DH), F32),
        ],
        compiler_params=params(),
        cost_estimate=cost(0, 2_000_000 * len(shapes)),
        name=name,
    )(queries, key_rows, value_rows, out_grad, plan_row)


def slice_kernel(me_ref, q_ref, k_ref, v_ref, g_ref, o_ref):
    o_ref[:, 0:QW] = q_ref[...]
    o_ref[:, QW : 2 * QW] = g_ref[...]
    o_ref[:, 2 * QW : 2 * QW + DH] = k_ref[...]
    o_ref[:, 2 * QW + DH : WIDE] = v_ref[...]


def slice_group(queries, key_rows, value_rows, out_grad, group):
    column = lambda i, g: (0, g[0])
    return pl.pallas_call(
        slice_kernel,
        grid_spec=pltpu.PrefetchScalarGridSpec(
            num_scalar_prefetch=1,
            grid=(1,),
            in_specs=[
                pl.BlockSpec((QUART, QW), column),
                pl.BlockSpec((QUART, DH), column),
                pl.BlockSpec((QUART, DH), column),
                pl.BlockSpec((QUART, QW), column),
            ],
            out_specs=pl.BlockSpec((QUART, WIDE), lambda i, g: (0, 0)),
        ),
        out_shape=jax.ShapeDtypeStruct((QUART, WIDE), BF16),
        compiler_params=params(),
        cost_estimate=cost(0, 1_800_000),
        name="slice_group",
    )(group.reshape(1), queries, key_rows, value_rows, out_grad)


def plan_lines(tail):
    total = SEQ * NBLK
    col = iota((1, total), 1).astype(F32)
    owner = jnp.floor((col + 0.5) * (1.0 / NBLK))
    place = col - owner * NBLK
    pick = (iota((DH, total), 0).astype(F32) == place).astype(BF16)
    mine = iota((SEQ, total), 0).astype(F32) == owner
    lines = []
    for row in (6, 7):
        spread = jnp.dot(tail[:, row, :].astype(BF16), pick, preferred_element_type=F32)
        lines.append(jnp.sum(jnp.where(mine, spread, 0.0), axis=0, keepdims=True))
    return lines


def low_choice(line):
    return (iota((64, line.shape[1]), 0).astype(F32) == line).astype(BF16)


def choose(sel, low, line, first, runs):
    for k in range(runs):
        row = jnp.where(line == float(first + k), 1.0, 0.0).astype(BF16)
        sel[k * 64 : (k + 1) * 64, :] = low * row


PARTS = 4
TILE = SEQ * NBLK // PARTS
RUNS = TILE // 64
SHARDS = TILE // NBLK


def route_kernel(in_ref, out_ref, xs, ks, sel, low):
    tail = in_ref[:, NBLK:SLOT, :].astype(F32)
    high, digits = plan_lines(tail)
    low[...] = low_choice(digits)
    here = iota((NBLK, DH), 1) // 16 == iota((NBLK, DH), 0) % 8
    fold = (iota((DH, DH), 0) % 16 == iota((DH, DH), 1) % 16).astype(BF16)
    xs[:, 0:DH] = in_ref[:, 0:NBLK, :].reshape(SEQ * NBLK, DH)
    for s in range(SEQ):
        rows = [jnp.broadcast_to(tail[s, b : b + 1, :], (8, DH)) for b in range(6)]
        wide = jnp.where(here, jnp.concatenate(rows, axis=0), 0.0).astype(BF16)
        ks[s * NBLK : (s + 1) * NBLK, :] = wide
    xs[:, DH : 2 * DH] = jnp.dot(ks[...], fold, preferred_element_type=F32).astype(BF16)
    for p in range(PARTS):
        choose(sel.at[p % 2], low[...], high, p * RUNS, RUNS)
        got = jnp.dot(sel[p % 2], xs[...], preferred_element_type=F32)
        for d in range(SHARDS):
            part = got[d * NBLK : (d + 1) * NBLK]
            kept = jnp.where(here, part[:, DH : 2 * DH], 0.0)
            sums = [jnp.sum(kept[b * 8 : b * 8 + 8], axis=0, keepdims=True) for b in range(6)]
            sums.append(jnp.zeros((2, DH), F32))
            out_ref[p * SHARDS + d, 0:NBLK, :] = part[:, 0:DH].astype(BF16)
            out_ref[p * SHARDS + d, NBLK:SLOT, :] = jnp.concatenate(sums, axis=0).astype(BF16)


def route(slots):
    vmem = pl.BlockSpec(memory_space=pltpu.VMEM)
    return pl.pallas_call(
        route_kernel,
        in_specs=[vmem],
        out_specs=vmem,
        out_shape=pltpu.HBM((SEQ, SLOT, DH), BF16),
        scratch_shapes=[
            pltpu.VMEM((SEQ * NBLK, 2 * DH), BF16),
            pltpu.VMEM((SEQ * NBLK, DH), BF16),
            pltpu.VMEM((2, TILE, SEQ * NBLK), BF16),
            pltpu.VMEM((64, SEQ * NBLK), BF16),
        ],
        compiler_params=params(SMALL_LIMIT),
        cost_estimate=cost(4 * SEQ * NBLK * SEQ * NBLK * DH, 2_000_000),
        name="route",
    )(slots)


def dot(a, b, dims):
    return lax.dot_general(a, b, (dims, ((), ())), preferred_element_type=F32)


NT = ((1,), (1,))
NN = ((1,), (0,))


def attend(q, g, k, v, k_cols, v_cols, allowed):
    scores = jnp.where(allowed, dot(k, q, NT) * (INV * LOG2E), NEG)
    weights = jnp.exp2(scores - jnp.max(scores, axis=0, keepdims=True))
    probs = weights * (1.0 / jnp.sum(weights, axis=0, keepdims=True))
    probs_low = probs.astype(BF16)
    grad_probs = dot(v, g, NT)
    centre = jnp.sum(probs * grad_probs, axis=0, keepdims=True)
    grad_scores = (probs * (grad_probs - centre) * INV).astype(BF16)
    out_cols = dot(v_cols, probs_low, NN)
    dq_cols = dot(k_cols, grad_scores, NN)
    return out_cols, dq_cols, dot(grad_scores, q, NN), dot(probs_low, g, NN)


def causal(seg_col, seg_row, first):
    j = iota((seg_col.shape[0], DH), 0)
    i = iota((seg_col.shape[0], DH), 1) + first
    return (seg_col == seg_row) & (j <= i)


PAD = 640
PAIR = 8


def stay_kernel(
    me_ref, q_any, k_any, v_any, g_any, plus, minus, two, col_ref, row_ref,
    out_ref, dq_ref, dk_ref, dv_ref, rows, kt, vt, dk, dv, sems,
):
    me = me_ref[0]

    def fetch(src, part):
        pltpu.make_async_copy(src, rows.at[pl.ds(part * QUART, QUART), :], sems.at[part]).start()

    wide = pl.ds(pl.multiple_of(me * QW, QW), QW)
    thin = pl.ds(pl.multiple_of(me * DH, DH), DH)

    def own(part):
        there = pl.ds(part * QUART, QUART)
        columns = (0, QW, 2 * QW, 2 * QW + DH, WIDE)
        for n, (src, at) in enumerate(((q_any, wide), (g_any, wide), (k_any, thin), (v_any, thin))):
            pltpu.make_async_copy(
                src.at[:, at], rows.at[there, columns[n] : columns[n + 1]], sems.at[part]
            ).start()

    @pl.when(me == 0)
    def _():
        own(0)
        fetch(minus, 1)
        fetch(two, 2)

    @pl.when(me == 1)
    def _():
        fetch(plus, 0)
        own(1)
        fetch(minus, 2)

    @pl.when(me == 2)
    def _():
        fetch(two, 0)
        fetch(plus, 1)
        own(2)

    @pl.when(me == 3)
    def _():
        fetch(minus, 0)
        fetch(two, 1)
        fetch(plus, 2)

    dk[...] = jnp.zeros_like(dk)
    dv[...] = jnp.zeros_like(dv)
    rows[STAY:PAD, :] = jnp.zeros((PAD - STAY, WIDE), BF16)
    for part in range(3):
        pltpu.make_async_copy(plus, rows.at[pl.ds(part * QUART, QUART), :], sems.at[part]).wait()
    kt[...] = rows[:, 2 * QW : 2 * QW + DH].astype(F32).T.astype(BF16)
    vt[...] = rows[:, 2 * QW + DH : WIDE].astype(F32).T.astype(BF16)

    for tile in range(PAD // DH):
        width = (tile + 1) * DH
        there = slice(tile * DH, width)
        count = min(DH, STAY - tile * DH)
        allowed = causal(col_ref[0:width, :], row_ref[:, there], tile * DH)
        allowed = jnp.concatenate([allowed] * PAIR, axis=1)

        for first in range(0, GROUP, PAIR):
            heads = range(first, first + PAIR)
            q = [rows[there, n * DH : (n + 1) * DH] for n in heads]
            g = [rows[there, QW + n * DH : QW + (n + 1) * DH] for n in heads]
            out, dq, dk_part, dv_part = attend(
                jnp.concatenate(q, axis=0),
                jnp.concatenate(g, axis=0),
                rows[0:width, 2 * QW : 2 * QW + DH],
                rows[0:width, 2 * QW + DH : WIDE],
                kt[:, 0:width],
                vt[:, 0:width],
                allowed,
            )
            for h, n in enumerate(heads):
                at = slice(n * DH, (n + 1) * DH)
                columns = slice(h * DH, (h + 1) * DH)
                out_ref[tile * DH : tile * DH + count, at] = out[:, columns].T[0:count].astype(BF16)
                dq_ref[tile * DH : tile * DH + count, at] = dq[:, columns].T[0:count].astype(BF16)
            dk[0:width, :] += dk_part
            dv[0:width, :] += dv_part

    dk_ref[...] = dk[0:STAY, :].astype(BF16)
    dv_ref[...] = dv[0:STAY, :].astype(BF16)


OUT_SHAPES = [
    jax.ShapeDtypeStruct((ROWS, QW), BF16),
    jax.ShapeDtypeStruct((ROWS, QW), BF16),
    jax.ShapeDtypeStruct((ROWS, DH), BF16),
    jax.ShapeDtypeStruct((ROWS, DH), BF16),
]


def attend_stay(me, held, received, seg_col, seg_row):
    any_spec = pl.BlockSpec(memory_space=pl.ANY)
    top = lambda n, m: (0, 0)
    return pl.pallas_call(
        stay_kernel,
        grid_spec=pltpu.PrefetchScalarGridSpec(
            num_scalar_prefetch=1,
            grid=(1,),
            in_specs=[any_spec] * 7 + [pl.BlockSpec((ROWS, 1), top), pl.BlockSpec((1, ROWS), top)],
            out_specs=[
                pl.BlockSpec((STAY, QW), top),
                pl.BlockSpec((STAY, QW), top),
                pl.BlockSpec((STAY, DH), top),
                pl.BlockSpec((STAY, DH), top),
            ],
            scratch_shapes=[
                pltpu.VMEM((PAD, WIDE), BF16),
                pltpu.VMEM((DH, PAD), BF16),
                pltpu.VMEM((DH, PAD), BF16),
                pltpu.VMEM((PAD, DH), F32),
                pltpu.VMEM((PAD, DH), F32),
                pltpu.SemaphoreType.DMA((3,)),
            ],
        ),
        out_shape=OUT_SHAPES,
        compiler_params=params(),
        cost_estimate=cost(60 * 2 * GROUP * STAY * STAY * DH, 6_000_000, GROUP * STAY * STAY),
        name="attend_stay",
    )(me.reshape(1), *held, *received, seg_col, seg_row)


SPAN = 2 * DH


def tail_kernel(
    slots, col_ref, row_ref, a0, a1, a2, a3, out_ref, dq_ref, dk_ref, dv_ref, qs, gs, ks, small
):
    pad = jnp.zeros((SPAN - QUART, DH), F32)
    for n in range(GROUP):
        qs[n, QUART:SPAN, :] = pad
        gs[n, QUART:SPAN, :] = pad
        for t in range(BLK):
            there = pl.ds(t, NBLK, stride=BLK)
            qs[n, there, :] = slots[t * GROUP + n, 0:NBLK, :].astype(F32)
            gs[n, there, :] = slots[SEQ // 2 + t * GROUP + n, 0:NBLK, :].astype(F32)
    small[...] = slots[:, NBLK:SLOT, :].astype(F32)
    pieces = [small[pl.ds(r * 8, 8), b, :][None] for r in range(8) for b in range(6)]
    plain = swap_groups(jnp.concatenate(pieces, axis=0))
    for r in range(8):
        ks[r // 4, pl.ds(r % 4, NBLK, stride=BLK), :] = plain[r * 6 : r * 6 + 6].reshape(NBLK, DH)
    for half in range(2):
        ks[half, QUART:SPAN, :] = pad
    for tile in range(2):
        first = tile * DH
        count = min(DH, QUART - first)
        there = slice(first, first + DH)
        k, v = ks[0, there, :], ks[1, there, :]
        allowed = causal(col_ref[there, :], row_ref[:, there], 0)
        out, dq, dk, dv = attend(
            qs[:, there, :].astype(BF16).reshape(QW, DH),
            gs[:, there, :].astype(BF16).reshape(QW, DH),
            k.astype(BF16),
            v.astype(BF16),
            k.T.astype(BF16),
            v.T.astype(BF16),
            jnp.concatenate([allowed] * GROUP, axis=1),
        )
        for n in range(GROUP):
            at = slice(n * DH, (n + 1) * DH)
            out_ref[first : first + count, at] = out[:, at].T[0:count].astype(BF16)
            dq_ref[first : first + count, at] = dq[:, at].T[0:count].astype(BF16)
        dk_ref[first : first + count, :] = dk[0:count].astype(BF16)
        dv_ref[first : first + count, :] = dv[0:count].astype(BF16)


def attend_tail(slots, seg_col, seg_row, partial):
    any_spec = pl.BlockSpec(memory_space=pl.ANY)
    last = lambda i: (3, 0)
    return pl.pallas_call(
        tail_kernel,
        grid=(1,),
        in_specs=[
            pl.BlockSpec((SEQ, SLOT, DH), lambda i: (0, 0, 0)),
            pl.BlockSpec((SPAN, 1), lambda i: (0, 0)),
            pl.BlockSpec((1, SPAN), lambda i: (0, 0)),
        ]
        + [any_spec] * 4,
        out_specs=[
            pl.BlockSpec((QUART, QW), last),
            pl.BlockSpec((QUART, QW), last),
            pl.BlockSpec((QUART, DH), last),
            pl.BlockSpec((QUART, DH), last),
        ],
        out_shape=OUT_SHAPES,
        input_output_aliases={3: 0, 4: 1, 5: 2, 6: 3},
        scratch_shapes=[
            pltpu.VMEM((GROUP, SPAN, DH), F32),
            pltpu.VMEM((GROUP, SPAN, DH), F32),
            pltpu.VMEM((2, SPAN, DH), F32),
            pltpu.VMEM((SEQ, 8, DH), F32),
        ],
        compiler_params=params(SMALL_LIMIT),
        cost_estimate=cost(6 * 2 * GROUP * QUART * DH * DH, 2_000_000, GROUP * QUART * DH),
        name="attend_tail",
    )(slots, seg_col, seg_row, *partial)


def after(values, *others):
    return lax.optimization_barrier((tuple(values), others))[0]


def on_device(queries, key_rows, value_rows, out_grad, mover_dest, segment_ids):
    me = lax.axis_index("head").astype(jnp.int32)
    held = (queries, key_rows, value_rows, out_grad)
    send = lambda x, *pairs: lax.ppermute(x, "head", list(pairs))
    exchange = lambda x: lax.all_to_all(x, "seq", split_axis=0, concat_axis=0, tiled=True)

    plan_row = mover_dest.reshape(1, NBLK)
    half = (SEQ // 2, SLOT, DH)
    one_lo, one_hi = pack(pack_one_kernel, "pack_one", 1, 1, [half] * 2, *held, plan_row)
    at_zero = send(one_lo, (3, 0))
    at_two = send(one_hi, (3, 2))
    rest = pack(pack_rest_kernel, "pack_rest", 4, 0, [(SEQ, SLOT, DH)] * 3, *held, plan_row)
    to_zero, to_two = send(rest[0], (3, 0)), send(rest[1], (3, 2))
    lo, hi = send(at_zero, (0, 1)), send(at_two, (2, 1))
    other = jnp.where(me == 3, rest[2], jnp.where(me == 0, to_zero, to_two))
    slots = jnp.where(me == 1, jnp.concatenate([lo, hi], axis=0), other)
    part = lambda shift: slice_group(*held, (me + shift) % 4)
    (slots, *slices) = after((slots, part(1), part(3), part(2)))

    pieces = exchange(slots)

    ahead, behind, across = after(slices, slots)
    two = send(across, (0, 2), (2, 0), (1, 3))
    plus = send(ahead, (0, 1), (1, 2), (2, 3))
    minus = send(behind, (1, 0), (2, 1), (0, 3))

    routed = route(pieces)
    stay = after((plus, minus, two), routed)
    seg_col = segment_ids.reshape(ROWS, 1)
    seg_row = segment_ids.reshape(1, ROWS)
    tail_seg = jnp.pad(segment_ids[STAY:], (0, SPAN - QUART), constant_values=-1)
    partial = attend_stay(me, held, stay, seg_col, seg_row)
    arrived = exchange(routed)
    return attend_tail(arrived, tail_seg.reshape(SPAN, 1), tail_seg.reshape(1, SPAN), partial)


def solution(mesh):
    rows = P(("seq", "head"), None)
    spread = P("seq", "head")
    return jax.shard_map(
        on_device,
        mesh=mesh,
        in_specs=(rows, rows, rows, rows, P("seq"), P("seq")),
        out_specs=(spread, spread, spread, spread),
        check_vma=False,
    )
```
